128 devices in a mesh: dp: 8 (over x, y_lo), tensor: 16 (over y_hi, z, core).
Axes of the slice: x: 4, y: 4 (y_hi: 2, y_lo: 2; y = y_hi * 2 + y_lo), z: 4, core: 2. Of those that a mesh axis runs over, the one named last changes fastest.
Arguments:
- tokens: bfloat16 [2560, 6144], P('dp', 'tensor'), may hold values from -6 to 6
- cotangent: bfloat16 [2560, 6144], P('dp', 'tensor'), may hold values from -6 to 6
- decor_matrix: float32 [6144, 6144], P('dp', 'tensor'), may hold values from -1 to 2
- in_weight: bfloat16 [6144, 12288], P(None, 'tensor'), may hold values from -0.078125 to 0.078125
- out_weight: bfloat16 [12288, 6144], P('tensor'), may hold values from -0.0546875 to 0.0546875
- lengths: int32 [8, 8], replicated, may hold values from 1 to 60, as said below
Outputs:
- layer_output: bfloat16 [2560, 6144], P('dp', 'tensor')
- input_grad: bfloat16 [2560, 6144], P('dp', 'tensor')
- decor_step: float32 [6144, 6144], P('dp', 'tensor')
The draws below stay inside these ranges and needn't reach their ends.
Inputs may be any that keep to these rules, and one draw needn't show every extreme that they name: `lengths`: each row sums to at most 320; exactly one row sums to 320; all rows together sum to 128 times the number of data ranks.
All inputs are finite; a program needn't handle non-finite values.
Results may differ from the reference program's by a relative error of at most 0.03.
Values may be sent and summed in bfloat16 or wider, within the bound.
No kernel may reach another device: no remote copies, remote signals or barrier semaphores. Data moves between devices by JAX's collectives and lax.ppermute only.
A program may use at most 128 MiB of HBM per device.

```python
import math
import jax
import jax.numpy as jnp
from jax import lax

D = 6144
FF = 12288
TOK_DEV = 320
SEQS = 8
MEAN = 128
TOKENS = 2560
N_DP = 8
N_TENSOR = 16


def draw_decor_matrix(key, part):
    first_key, second_key = jax.random.split(jax.random.fold_in(key, 11))
    off_part = jax.random.normal(first_key, (D, D), jnp.float32) * (0.5 / math.sqrt(D))
    main_part = jax.random.uniform(second_key, (D,), jnp.float32, 0.8, 1.25)
    return off_part + jnp.eye(D, dtype=jnp.float32) * main_part[None, :]


def draw_lengths(key, part):
    first_key, second_key, third_key, fourth_key = jax.random.split(jax.random.fold_in(key, 23), 4)
    remaining = N_DP * MEAN - TOK_DEV
    base_count = remaining // (N_DP - 1)
    extra_count = remaining - base_count * (N_DP - 1)
    jitter = jax.random.randint(first_key, (N_DP - 1,), 0, base_count // 2)
    others = base_count + jitter - jnp.roll(jitter, 1)
    others = others.at[0].add(extra_count)
    live_values = jnp.concatenate([jnp.full((1,), TOK_DEV, jnp.int32), others.astype(jnp.int32)])
    order = jax.random.permutation(second_key, N_DP)
    live_counts = jnp.zeros((N_DP,), jnp.int32).at[order].set(live_values)
    each_count = live_counts // SEQS
    spare_count = live_counts - each_count * SEQS
    raw_bits = jax.random.randint(third_key, (N_DP, SEQS), 0, 1000000)
    wiggle = raw_bits % jnp.maximum(each_count // 4, 1)[:, None]
    seq_lengths = each_count[:, None] + wiggle - jnp.roll(wiggle, 1, axis=1)
    seq_lengths = seq_lengths.at[:, 0].add(spare_count)
    longest = TOK_DEV // SEQS + TOK_DEV // (2 * SEQS)
    rest_total = TOK_DEV - longest
    rest_each = rest_total // (SEQS - 1)
    rest_spare = rest_total - rest_each * (SEQS - 1)
    rest_bits = jax.random.randint(fourth_key, (SEQS - 1,), 0, 1000000)
    rest_wiggle = rest_bits % max(rest_each // 4, 1)
    tail_lengths = rest_each + rest_wiggle - jnp.roll(rest_wiggle, 1)
    tail_lengths = tail_lengths.at[0].add(rest_spare)
    full_row = jnp.concatenate([jnp.full((1,), longest, jnp.int32), tail_lengths.astype(jnp.int32)])
    is_full = jnp.arange(N_DP, dtype=jnp.int32) == order[0]
    seq_lengths = jnp.where(is_full[:, None], full_row[None, :], seq_lengths)
    return seq_lengths.astype(jnp.int32)


def level_of(stream_key, shape, shards, low, top_value):
    def one(dim, parts):
        heights = jax.random.uniform(jax.random.fold_in(jax.random.fold_in(stream_key, 6), dim), (parts,), jnp.float32, low / len(shards), top_value / len(shards))
        return jnp.repeat(jnp.exp(heights), shape[dim] // parts).reshape((-1,) + (1,) * (len(shape) - dim - 1))

    loudness = one(*shards[0])
    for cut in shards[1:]:
        loudness = loudness * one(*cut)
    return loudness


def normal_values(stream_key, extent, width, bound, cuts=(), held_as=jnp.bfloat16):
    entries = width * jax.random.normal(stream_key, extent, jnp.float32)
    if cuts:
        entries = entries * level_of(stream_key, extent, cuts, -0.22, 0.18)
    return jnp.clip(entries, -bound, bound).astype(held_as)


def setup_inputs(seed: int = 0) -> dict:
    splits = jax.random.split(jax.random.key(seed), 7)
    tokens = normal_values(splits[0], (TOKENS, D), 1.0, 6.0, ((0, 8), (1, 16)))
    cotangent = normal_values(splits[1], (TOKENS, D), 1.0, 6.0, ((0, 8), (1, 16)))
    decor_matrix = draw_decor_matrix(jax.random.fold_in(splits[6], 71), 0)
    in_weight = normal_values(splits[3], (D, FF), D ** -0.5, 0.078125, ((1, 16),))
    out_weight = normal_values(splits[4], (FF, D), FF ** -0.5, 0.0546875, ((0, 16),))
    lengths = draw_lengths(jax.random.fold_in(splits[6], 71), 0)
    return {"tokens": tokens, "cotangent": cotangent, "decor_matrix": decor_matrix, "in_weight": in_weight, "out_weight": out_weight, "lengths": lengths}


GELU_SCALE = math.sqrt(2.0 / math.pi)
GELU_CUBIC = 0.044715
EXACT_PRECISION = lax.Precision.HIGHEST
CONTRACT_LAST = (((1,), (1,)), ((), ()))
CONTRACT_FIRST = (((0,), (0,)), ((), ()))

def gelu_pair(values):
    inner_arg = GELU_SCALE * (values + GELU_CUBIC * values * values * values)
    tangent = jnp.tanh(inner_arg)
    output = 0.5 * values * (1.0 + tangent)
    gelu_slope = 0.5 * (1.0 + tangent) + 0.5 * values * (1.0 - tangent * tangent) * GELU_SCALE * (1.0 + 3.0 * GELU_CUBIC * values * values)
    return (output, gelu_slope)

def token_weights(lengths, rank_list, row_count, spread):
    flat_lengths = lengths.reshape(-1)
    live_counts = lax.optimization_barrier(jnp.sum(lengths, axis=1))
    rank_starts = jnp.cumsum(live_counts) - live_counts
    local_index = jnp.arange(row_count, dtype=jnp.int32)
    if spread:
        packed_index = rank_list[:, None] * row_count + local_index[None, :]
        is_valid = packed_index >= 0
    else:
        rank_match = rank_list[:, None] == jnp.arange(lengths.shape[0], dtype=jnp.int32)[None, :]
        rank_start = lax.optimization_barrier(jnp.sum(jnp.where(rank_match, rank_starts[None, :], 0), axis=1))
        rank_limit = lax.optimization_barrier(jnp.sum(jnp.where(rank_match, live_counts[None, :], 0), axis=1))
        packed_index = rank_start[:, None] + local_index[None, :]
        is_valid = local_index[None, :] < rank_limit[:, None]
    packed_index = packed_index.reshape(-1)
    seq_ends = jnp.cumsum(flat_lengths)
    seq_starts = seq_ends - flat_lengths
    member = (packed_index[:, None] >= seq_starts[None, :]) & (packed_index[:, None] < seq_ends[None, :])
    seq_share = 1.0 / (lengths.shape[1] * flat_lengths.astype(jnp.float32))
    weight = lax.optimization_barrier(jnp.sum(jnp.where(member, seq_share[None, :], 0.0), axis=1))
    is_valid = is_valid.reshape(-1)
    return (jnp.where(is_valid, weight, 0.0), is_valid)

def block_sum(left_blocks, right_blocks, dimension_numbers, row_total, col_total, precision):

    def add_block(running, blocks_pair):
        block_term = lax.dot_general(blocks_pair[0], blocks_pair[1], dimension_numbers, precision=precision, preferred_element_type=jnp.float32)
        return (running + lax.optimization_barrier(block_term.astype(jnp.bfloat16)).astype(jnp.float32), None)
    start_value = jnp.zeros((row_total, col_total), jnp.float32)
    summed, _ = lax.scan(add_block, start_value, (left_blocks, right_blocks))
    return summed

def reference(tokens, cotangent, decor_matrix, in_weight, out_weight, lengths):
    weights, inside = token_weights(lengths, jnp.arange(N_DP, dtype=jnp.int32), TOK_DEV, False)
    feature_width = D // N_TENSOR
    hidden_width = FF // N_TENSOR
    row_total = tokens.shape[0]
    token_blocks = jnp.transpose(tokens.astype(jnp.float32).reshape(row_total, N_TENSOR, feature_width), (1, 0, 2))
    decor_blocks = jnp.transpose(decor_matrix.reshape(D, N_TENSOR, feature_width), (1, 0, 2))
    summed = block_sum(token_blocks, decor_blocks, CONTRACT_LAST, row_total, D, EXACT_PRECISION)
    whitened = summed.astype(jnp.bfloat16)
    pre_act = jnp.dot(whitened, in_weight, preferred_element_type=jnp.float32)
    gelu_out, gelu_slope = gelu_pair(pre_act)
    hidden = gelu_out.astype(jnp.bfloat16)
    hidden_blocks = jnp.transpose(hidden.reshape(row_total, N_TENSOR, hidden_width), (1, 0, 2))
    out_blocks = out_weight.reshape(N_TENSOR, hidden_width, D)
    out_sum = block_sum(hidden_blocks, out_blocks, (((1,), (0,)), ((), ())), row_total, D, None)
    valid_column = inside[:, None]
    layer_output = jnp.where(valid_column, out_sum, 0.0).astype(jnp.bfloat16)
    back_hidden = jnp.dot(cotangent, out_weight.T, preferred_element_type=jnp.float32)
    delta_hidden = (back_hidden * gelu_slope).astype(jnp.bfloat16)
    delta_blocks = jnp.transpose(delta_hidden.reshape(row_total, N_TENSOR, hidden_width), (1, 0, 2))
    in_blocks = jnp.transpose(in_weight.reshape(D, N_TENSOR, hidden_width), (1, 0, 2))
    grad_sum = block_sum(delta_blocks, in_blocks, CONTRACT_LAST, row_total, D, None)
    input_grad = jnp.where(valid_column, grad_sum, 0.0).astype(jnp.bfloat16)
    dense_whitened = whitened.astype(jnp.float32)
    mixed_rows = jnp.dot(dense_whitened, decor_matrix, precision=EXACT_PRECISION, preferred_element_type=jnp.float32)
    weighted_mixed = mixed_rows * weights[:, None]
    product = lax.dot_general(dense_whitened, weighted_mixed, CONTRACT_FIRST, precision=EXACT_PRECISION, preferred_element_type=jnp.float32)
    diagonal = lax.optimization_barrier(jnp.sum(weights[:, None] * dense_whitened * dense_whitened, axis=0))
    decor_step = product - diagonal[:, None] * decor_matrix
    return (layer_output, input_grad, decor_step)
```

```python
import math

import jax
import jax.numpy as jnp
from jax import lax
from jax.sharding import Mesh, PartitionSpec as P

GELU_SCALE = math.sqrt(2.0 / math.pi)
GELU_CUBIC = 0.044715
BF16 = jnp.bfloat16
F32 = jnp.float32
CONTRACT_LAST = (((1,), (1,)), ((), ()))
CONTRACT_FIRST = (((0,), (0,)), ((), ()))
DP = ("x", "yl")
CHIPS = ("yh", "z")
CORE = "core"
N_DP = 8
N_CHIP = 8
GROUP = 128
PART = 8


def gelu_pair(values):
    inner_arg = GELU_SCALE * (values + GELU_CUBIC * values * values * values)
    tangent = jnp.tanh(inner_arg)
    output = 0.5 * values * (1.0 + tangent)
    gelu_slope = 0.5 * (1.0 + tangent) + 0.5 * values * (1.0 - tangent * tangent) * GELU_SCALE * (
        1.0 + 3.0 * GELU_CUBIC * values * values
    )
    return (output, gelu_slope)


def packed_weights(lengths, packed_index):
    flat_lengths = lengths.reshape(-1)
    seq_ends = jnp.cumsum(flat_lengths)
    seq_starts = seq_ends - flat_lengths
    member = (packed_index[:, None] >= seq_starts[None, :]) & (
        packed_index[:, None] < seq_ends[None, :]
    )
    seq_share = 1.0 / (lengths.shape[1] * flat_lengths.astype(F32))
    return jnp.sum(jnp.where(member, seq_share[None, :], 0.0), axis=1)


def split_bf16(values):
    high = lax.reduce_precision(values, 8, 7)
    return (high.astype(BF16), (values - high).astype(BF16))


def dot(left, right, numbers=(((1,), (0,)), ((), ()))):
    return lax.dot_general(left, right, numbers, preferred_element_type=F32)


def swap_core(value):
    return lax.ppermute(value, CORE, [(0, 1), (1, 0)])


def local(tokens, cotangent, decor_matrix, in_weight, out_weight, lengths):
    row_total, width = tokens.shape
    own_rank = lax.axis_index(DP)
    core = lax.axis_index(CORE)
    first_core = core == 0

    other_matrix = swap_core(decor_matrix)

    live = jnp.sum(lengths, axis=1)
    starts = jnp.cumsum(live) - live
    own_start = lax.dynamic_index_in_dim(starts, own_rank, keepdims=False)
    own_live = lax.dynamic_index_in_dim(live, own_rank, keepdims=False)

    local_row = jnp.arange(row_total, dtype=jnp.int32)
    own_packed = jnp.where(local_row < own_live, own_start + local_row, -1)
    all_packed = jnp.where(
        local_row[None, :] < live[:, None], starts[:, None] + local_row[None, :], -1
    ).reshape(-1)

    half_row = jnp.arange(N_CHIP * N_DP * PART, dtype=jnp.int32)
    half_base = (
        (half_row // PART) % N_DP * GROUP
        + half_row // (PART * N_DP) * (2 * PART)
        + half_row % PART
    )
    own_half = half_base + core * PART
    other_half = half_base + (1 - core) * PART

    pack = (jnp.arange(N_DP * GROUP, dtype=jnp.int32)[:, None] == own_packed[None, :]).astype(BF16)
    cot_placed = dot(pack, cotangent).astype(BF16).reshape(N_DP, GROUP, width)
    sent = jnp.concatenate(
        [jnp.broadcast_to(tokens[None], (N_DP,) + tokens.shape), cot_placed], axis=1
    )
    got = lax.all_to_all(sent, DP, 0, 0, tiled=True)
    all_tokens = got[:, :row_total].reshape(N_DP * row_total, width)
    cot_packed = jnp.sum(got[:, row_total:].astype(F32), axis=0).astype(BF16)

    pick_own = (own_half[:, None] == all_packed[None, :]).astype(BF16)
    pick_other = (other_half[:, None] == all_packed[None, :]).astype(BF16)
    far_tokens = swap_core(dot(pick_other, all_tokens).astype(BF16))
    near_tokens = dot(pick_own, all_tokens).astype(BF16)

    own_high, own_low = split_bf16(decor_matrix)
    far_high, far_low = split_bf16(other_matrix)
    partial_white = (
        dot(near_tokens, own_high, CONTRACT_LAST)
        + dot(near_tokens, own_low, CONTRACT_LAST)
        + dot(far_tokens, far_high, CONTRACT_LAST)
        + dot(far_tokens, far_low, CONTRACT_LAST)
    ).astype(BF16)

    chunk = N_DP * PART
    partial_white = partial_white.reshape(N_CHIP, chunk, 2 * width)
    sent = jnp.concatenate(
        [
            partial_white[:, :, :width],
            partial_white[:, :, width:],
            jnp.broadcast_to(cot_packed[None], (N_CHIP,) + cot_packed.shape),
        ],
        axis=1,
    )
    got = lax.all_to_all(sent, CHIPS, 0, 0, tiled=True)
    cot_near = got[:, 2 * chunk :]
    cot_far = swap_core(cot_near)
    white_sum = jnp.sum(got[:, : 2 * chunk].astype(F32), axis=0).astype(BF16)
    white_chunk = jnp.concatenate([white_sum[:chunk], white_sum[chunk:]], axis=1)

    white_part = lax.all_to_all(
        white_chunk.reshape(N_DP, PART, 2 * width), DP, 0, 0, tiled=True
    ).reshape(chunk, 2 * width)

    sent = jnp.broadcast_to(
        jnp.concatenate([white_part, white_chunk], axis=0)[None], (N_CHIP, 2 * chunk, 2 * width)
    )
    near = lax.all_to_all(sent, CHIPS, 0, 0, tiled=True)
    far = swap_core(near)

    white_rows = jnp.concatenate([near[:, chunk:], far[:, chunk:]], axis=0).reshape(
        N_DP * GROUP, 2 * width
    )
    row_weights = packed_weights(lengths, jnp.concatenate([own_half, other_half]))
    mixed_part = (dot(white_rows, own_high) + dot(white_rows, own_low)).astype(BF16)
    mixed_got = lax.all_to_all(mixed_part.reshape(N_DP, GROUP, width), DP, 0, 0, tiled=True)
    mixed_own = jnp.sum(mixed_got.astype(F32), axis=0).astype(BF16)
    white_float = white_rows.astype(F32)
    diagonal = jnp.sum(row_weights[:, None] * white_float * white_float, axis=0)

    def rows_of(block):
        block = block.reshape(N_CHIP, N_DP, PART, 2 * width)
        return jnp.transpose(block, (0, 2, 1, 3)).reshape(N_CHIP, PART, N_DP * 2 * width)

    ff_near, ff_far = rows_of(near[:, :chunk]), rows_of(far[:, :chunk])
    whitened = jnp.stack(
        [jnp.where(first_core, ff_near, ff_far), jnp.where(first_core, ff_far, ff_near)], axis=1
    ).reshape(GROUP, N_DP * 2 * width)
    cot_pair = jnp.stack(
        [jnp.where(first_core, cot_near, cot_far), jnp.where(first_core, cot_far, cot_near)], axis=1
    )
    cot_full = jnp.transpose(cot_pair, (2, 0, 1, 3)).reshape(GROUP, N_CHIP * 2 * width)

    pre_act = dot(whitened, in_weight)
    gelu_out, gelu_slope = gelu_pair(pre_act)
    hidden = gelu_out.astype(BF16)
    back_hidden = dot(cot_full, out_weight, CONTRACT_LAST)
    delta_hidden = (back_hidden * gelu_slope).astype(BF16)
    out_partial = dot(hidden, out_weight).astype(BF16)
    grad_partial = dot(delta_hidden, in_weight, CONTRACT_LAST).astype(BF16)

    both = jnp.stack([out_partial, grad_partial]).reshape(2, GROUP, N_CHIP, 2, width)
    kept = lax.dynamic_index_in_dim(both, core, 3, keepdims=False)
    given = lax.dynamic_index_in_dim(both, 1 - core, 3, keepdims=False)
    summed = (kept.astype(F32) + swap_core(given).astype(F32)).astype(BF16)
    sent = jnp.transpose(summed, (2, 0, 1, 3)).reshape(N_CHIP, 2 * GROUP, width)
    got = lax.all_to_all(sent, CHIPS, 0, 0, tiled=True)
    out_own = jnp.sum(got.astype(F32), axis=0).astype(BF16)

    sent = jnp.concatenate([out_own, mixed_own], axis=0)
    sent = jnp.broadcast_to(sent[None], (N_DP,) + sent.shape)
    got = lax.all_to_all(sent, DP, 0, 0, tiled=True)
    mixed = got[:, 2 * GROUP :].reshape(N_DP * GROUP, width)
    weighted_mixed = (mixed.astype(F32) * row_weights[:, None]).astype(BF16)
    product = dot(white_rows, weighted_mixed, CONTRACT_FIRST)
    decor_step = product - diagonal[:, None] * decor_matrix

    unpack = (own_packed[:, None] == jnp.arange(N_DP * GROUP, dtype=jnp.int32)[None, :]).astype(BF16)
    out_rows = dot(unpack, got[:, :GROUP].reshape(N_DP * GROUP, width)).astype(BF16)
    grad_rows = dot(unpack, got[:, GROUP : 2 * GROUP].reshape(N_DP * GROUP, width)).astype(BF16)
    return (out_rows, grad_rows, decor_step)


def solution(mesh):
    fine = Mesh(mesh.devices.reshape(4, 2, 2, 4, 2), ("x", "yl", "yh", "z", "core"))
    tensor = ("yh", "z", "core")
    placed = (
        P(DP, tensor),
        P(DP, tensor),
        P(DP, tensor),
        P(None, tensor),
        P(tensor, None),
        P(),
    )
    return jax.shard_map(
        local,
        mesh=fine,
        in_specs=placed,
        out_specs=(P(DP, tensor), P(DP, tensor), P(DP, tensor)),
        check_vma=False,
    )
```

```python
import math

import jax
import jax.numpy as jnp
from jax import lax
from jax.experimental import pallas as pl
from jax.experimental.pallas import tpu as pltpu
from jax.sharding import Mesh, PartitionSpec as P

GELU_SCALE = math.sqrt(2.0 / math.pi)
GELU_CUBIC = 0.044715
BF16 = jnp.bfloat16
F32 = jnp.float32
CONTRACT_LAST = (((1,), (1,)), ((), ()))
CONTRACT_FIRST = (((0,), (0,)), ((), ()))
DP = ("x", "yl")
CHIPS = ("yh", "z")
CORE = "core"
N_DP = 8
N_CHIP = 8
GROUP = 128
PART = 8
HALF = 64
ROWS = 1024
CHUNK = 768
SLOTS = 48
WEIGHT_COPIES = 4


def gelu_pair(values):
    inner_arg = GELU_SCALE * (values + GELU_CUBIC * values * values * values)
    tangent = jnp.tanh(inner_arg)
    output = 0.5 * values * (1.0 + tangent)
    gelu_slope = 0.5 * (1.0 + tangent) + 0.5 * values * (1.0 - tangent * tangent) * GELU_SCALE * (
        1.0 + 3.0 * GELU_CUBIC * values * values
    )
    return (output, gelu_slope)


def packed_weights(lengths, packed_index):
    flat_lengths = lengths.reshape(-1)
    seq_ends = jnp.cumsum(flat_lengths)
    seq_starts = seq_ends - flat_lengths
    member = (packed_index[:, None] >= seq_starts[None, :]) & (
        packed_index[:, None] < seq_ends[None, :]
    )
    seq_share = 1.0 / (lengths.shape[1] * flat_lengths.astype(F32))
    return jnp.sum(jnp.where(member, seq_share[None, :], 0.0), axis=1)


def split_bf16(values):
    high = lax.reduce_precision(values, 8, 7)
    return (high.astype(BF16), (values - high).astype(BF16))


def dot(left, right, numbers=(((1,), (0,)), ((), ()))):
    return lax.dot_general(left, right, numbers, preferred_element_type=F32)


def swap_core(value):
    return lax.ppermute(value, CORE, [(0, 1), (1, 0)])


def mixed_kernel(core_ref, near_ref, far_ref, high_ref, low_ref, rows_ref, mixed_ref):
    own = pl.multiple_of(core_ref[0] * HALF, HALF)
    other = pl.multiple_of(HALF - core_ref[0] * HALF, HALF)
    for group in range(N_DP):
        columns = pl.ds(group * CHUNK, CHUNK)
        rows_ref[group, pl.ds(own, HALF), :] = near_ref[:, columns]
        rows_ref[group, pl.ds(other, HALF), :] = far_ref[:, columns]
    rows = rows_ref[...].reshape(ROWS, CHUNK)
    total = dot(rows, high_ref[...]) + dot(rows, low_ref[...])
    mixed_ref[...] = total.astype(BF16).reshape(mixed_ref.shape)


def mixed_terms(core, near, far, high, low):
    vmem = pl.BlockSpec(memory_space=pltpu.VMEM)
    return pl.pallas_call(
        mixed_kernel,
        in_specs=[pl.BlockSpec(memory_space=pltpu.SMEM)] + [vmem] * 4,
        out_specs=[vmem, vmem],
        out_shape=[
            jax.ShapeDtypeStruct((N_DP, GROUP, CHUNK), BF16),
            jax.ShapeDtypeStruct((N_DP, GROUP, high.shape[1]), BF16),
        ],
        compiler_params=pltpu.CompilerParams(vmem_limit_bytes=16 << 20),
        cost_estimate=pl.CostEstimate(
            flops=4 * ROWS * CHUNK * 384, bytes_accessed=5 << 20, transcendentals=0
        ),
        name="mixed_terms",
    )(core, near, far, high, low)


def feed_kernel(
    core_ref, near_ref, far_ref, cot_near_ref, cot_far_ref, in_ref, out_ref, kept_ref, given_ref,
    in_buf, out_buf, rows_buf, cot_buf, hidden_buf, delta_buf, in_sem, out_sem,
):
    own = pl.multiple_of(core_ref[0] * HALF, HALF)
    other = pl.multiple_of(HALF - core_ref[0] * HALF, HALF)
    first_core = core_ref[0] == 0
    steps = kept_ref.shape[0]
    width = CHUNK // 2
    in_copies, out_copies = [], []
    for step in range(WEIGHT_COPIES):
        rows = pl.ds(step * (in_buf.shape[0] // WEIGHT_COPIES), in_buf.shape[0] // WEIGHT_COPIES)
        in_copies.append(
            pltpu.make_async_copy(in_ref.at[rows, :], in_buf.at[rows, :], in_sem.at[step])
        )
        columns = pl.ds(
            step * (out_buf.shape[1] // WEIGHT_COPIES), out_buf.shape[1] // WEIGHT_COPIES
        )
        out_copies.append(
            pltpu.make_async_copy(out_ref.at[:, columns], out_buf.at[:, columns], out_sem.at[step])
        )
    for step in range(WEIGHT_COPIES):
        out_copies[step].start()
        in_copies[step].start()
    rows_buf[pl.ds(own, HALF), :] = near_ref[...]
    rows_buf[pl.ds(other, HALF), :] = far_ref[...]
    for step in range(steps):
        for half in range(2):
            lanes = pl.ds(half * width, width)
            close, away = cot_near_ref[step, :, lanes], cot_far_ref[step, :, lanes]
            rows = pl.ds(half * HALF, HALF)
            cot_buf[rows, pl.ds(step * CHUNK, width)] = jnp.where(first_core, close, away)
            cot_buf[rows, pl.ds(step * CHUNK + width, width)] = jnp.where(first_core, away, close)
    pre_act, back = 0.0, 0.0
    depth = in_buf.shape[0] // WEIGHT_COPIES
    for step in range(WEIGHT_COPIES):
        span = pl.ds(step * depth, depth)
        out_copies[step].wait()
        back = back + dot(cot_buf[:, span], out_buf[:, span], CONTRACT_LAST)
        in_copies[step].wait()
        pre_act = pre_act + dot(rows_buf[:, span], in_buf[span, :])
    gelu_out, gelu_slope = gelu_pair(pre_act)
    hidden_buf[...] = gelu_out.astype(BF16)
    delta_buf[...] = (back * gelu_slope).astype(BF16)

    def store(step, place, value):
        left, right = value[:, :width], value[:, width:]
        rows = pl.ds(place, GROUP)
        kept_ref[step, rows, :] = jnp.where(first_core, left, right).astype(BF16)
        given_ref[step, rows, :] = jnp.where(first_core, right, left).astype(BF16)

    for step in range(steps):
        columns = pl.ds(step * CHUNK, CHUNK)
        store(step, GROUP, dot(delta_buf[...], in_buf[columns, :], CONTRACT_LAST))
    for step in range(steps):
        columns = pl.ds(step * CHUNK, CHUNK)
        store(step, 0, dot(hidden_buf[...], out_buf[:, columns]))


def feed_forward(core, near, far, cot_near, cot_far, in_weight, out_weight):
    vmem = pl.BlockSpec(memory_space=pltpu.VMEM)
    anywhere = pl.BlockSpec(memory_space=pl.ANY)
    steps = in_weight.shape[0] // CHUNK
    hidden = in_weight.shape[1]
    part = jax.ShapeDtypeStruct((steps, 2 * GROUP, CHUNK // 2), BF16)
    return pl.pallas_call(
        feed_kernel,
        in_specs=[pl.BlockSpec(memory_space=pltpu.SMEM)] + [vmem] * 4 + [anywhere] * 2,
        out_specs=[vmem, vmem],
        out_shape=[part, part],
        scratch_shapes=[
            pltpu.VMEM(in_weight.shape, BF16),
            pltpu.VMEM(out_weight.shape, BF16),
            pltpu.VMEM((GROUP, steps * CHUNK), BF16),
            pltpu.VMEM((GROUP, steps * CHUNK), BF16),
            pltpu.VMEM((GROUP, hidden), BF16),
            pltpu.VMEM((GROUP, hidden), BF16),
            pltpu.SemaphoreType.DMA((WEIGHT_COPIES,)),
            pltpu.SemaphoreType.DMA((WEIGHT_COPIES,)),
        ],
        compiler_params=pltpu.CompilerParams(vmem_limit_bytes=46 << 20),
        cost_estimate=pl.CostEstimate(flops=1 << 20, bytes_accessed=1 << 16, transcendentals=0),
        name="feed_forward",
    )(core, near, far, cot_near, cot_far, in_weight, out_weight)


def rank_spans(lengths_ref):
    live, starts, total = [], [], 0
    for rank in range(N_DP):
        count = lengths_ref[rank, 0]
        for column in range(1, lengths_ref.shape[1]):
            count = count + lengths_ref[rank, column]
        live.append(count)
        starts.append(total)
        total = total + count
    return live, starts


def entry_of(values, rank):
    found = values[0]
    for place in range(1, N_DP):
        found = jnp.where(rank == place, values[place], found)
    return found


def first_row(group, start):
    return lax.rem(group + ROWS - start, N_DP)


def one_hot(condition):
    return condition.astype(F32).astype(BF16)


def pack_kernel(place_ref, lengths_ref, tokens_ref, cot_ref, sent_ref):
    live, starts = rank_spans(lengths_ref)
    start, own_live = entry_of(starts, place_ref[0]), entry_of(live, place_ref[0])
    row_total, width = tokens_ref.shape
    slot = lax.broadcasted_iota(jnp.int32, (SLOTS, row_total), 0)
    row = lax.broadcasted_iota(jnp.int32, (SLOTS, row_total), 1)
    for group in range(N_DP):
        wanted = slot * N_DP + first_row(group, start)
        pick = one_hot((row == wanted) & (row < own_live))
        sent_ref[group, :, pl.ds(0, width)] = dot(pick, tokens_ref[...]).astype(BF16)
        sent_ref[group, :, pl.ds(width, width)] = dot(pick, cot_ref[...]).astype(BF16)


def group_kernel(place_ref, lengths_ref, got_ref, near_ref, given_ref, cot_ref, rows_buf):
    live, starts = rank_spans(lengths_ref)
    group, core = place_ref[0], place_ref[1]
    row = lax.broadcasted_iota(jnp.int32, (GROUP, SLOTS), 0)
    slot = lax.broadcasted_iota(jnp.int32, (GROUP, SLOTS), 1)
    total = jnp.zeros((GROUP, CHUNK), F32)
    for rank in range(N_DP):
        first = first_row(group, starts[rank])
        shift = (starts[rank] + first - group) // N_DP
        pick = one_hot((row == slot + shift) & (slot * N_DP + first < live[rank]))
        total = total + dot(pick, got_ref[rank])
    rows_buf[...] = total.astype(BF16)
    width = CHUNK // 2
    left, right = pl.ds(0, width), pl.ds(width, width)
    near_ref[...] = rows_buf[pl.ds(pl.multiple_of(core * HALF, HALF), HALF), left]
    given_ref[...] = rows_buf[pl.ds(pl.multiple_of(HALF - core * HALF, HALF), HALF), left]
    cot_ref[:, left] = rows_buf[pl.ds(0, HALF), right]
    cot_ref[:, right] = rows_buf[pl.ds(HALF, HALF), right]


def spread_kernel(place_ref, lengths_ref, got_ref, mixed_ref, sent_ref, rows_buf):
    live, starts = rank_spans(lengths_ref)
    group = place_ref[0]
    total = got_ref[0].astype(F32)
    for chip in range(1, N_CHIP):
        total = total + got_ref[chip].astype(F32)
    rows_buf[...] = total.astype(BF16)
    slot = lax.broadcasted_iota(jnp.int32, (SLOTS, GROUP), 0)
    row = lax.broadcasted_iota(jnp.int32, (SLOTS, GROUP), 1)
    for rank in range(N_DP):
        first = first_row(group, starts[rank])
        shift = (starts[rank] + first - group) // N_DP
        pick = one_hot((row == slot + shift) & (slot * N_DP + first < live[rank]))
        for half in range(2):
            rows = rows_buf[pl.ds(half * GROUP, GROUP), :]
            sent_ref[rank, pl.ds(half * SLOTS, SLOTS), :] = dot(pick, rows).astype(BF16)
        sent_ref[rank, pl.ds(2 * SLOTS, GROUP), :] = mixed_ref[...]


def final_kernel(
    place_ref, lengths_ref, got_ref, rows_ref, diagonal_ref, matrix_ref, out_ref, grad_ref, step_ref
):
    live, starts = rank_spans(lengths_ref)
    start, own_live = entry_of(starts, place_ref[0]), entry_of(live, place_ref[0])
    row_total, width = out_ref.shape
    row = lax.broadcasted_iota(jnp.int32, (row_total, SLOTS), 0)
    slot = lax.broadcasted_iota(jnp.int32, (row_total, SLOTS), 1)
    out_total = jnp.zeros((row_total, width), F32)
    grad_total = jnp.zeros((row_total, width), F32)
    for group in range(N_DP):
        wanted = slot * N_DP + first_row(group, start)
        pick = one_hot((row == wanted) & (row < own_live))
        out_total = out_total + dot(pick, got_ref[group, pl.ds(0, SLOTS), :])
        grad_total = grad_total + dot(pick, got_ref[group, pl.ds(SLOTS, SLOTS), :])
    out_ref[...] = out_total.astype(BF16)
    grad_ref[...] = grad_total.astype(BF16)
    mixed = got_ref[:, pl.ds(2 * SLOTS, GROUP), :].reshape(ROWS, width)
    product = dot(rows_ref[...], mixed, CONTRACT_FIRST)
    step_ref[...] = product - diagonal_ref[...] * matrix_ref[...]


def small_call(kernel, shapes, scratch, limit, *operands):
    smem = pl.BlockSpec(memory_space=pltpu.SMEM)
    vmem = pl.BlockSpec(memory_space=pltpu.VMEM)
    return pl.pallas_call(
        kernel,
        in_specs=[smem, smem] + [vmem] * (len(operands) - 2),
        out_specs=[vmem] * len(shapes),
        out_shape=shapes,
        scratch_shapes=scratch,
        compiler_params=pltpu.CompilerParams(vmem_limit_bytes=limit << 20),
        cost_estimate=pl.CostEstimate(flops=1 << 20, bytes_accessed=1 << 16, transcendentals=0),
        name=kernel.__name__,
    )(*operands)


def local(tokens, cotangent, decor_matrix, in_weight, out_weight, lengths):
    width = tokens.shape[1]
    own_rank = lax.axis_index(DP)
    core = lax.axis_index(CORE)
    core_list = core.reshape(1)
    place = jnp.stack([own_rank, core])

    def bf16_shape(*shape):
        return jax.ShapeDtypeStruct(shape, BF16)

    (sent,) = small_call(
        pack_kernel, [bf16_shape(N_DP, SLOTS, CHUNK)], [], 8, place, lengths, tokens, cotangent
    )
    got = lax.all_to_all(sent, DP, 0, 0, tiled=True)
    near_tokens, given_tokens, cot_packed = small_call(
        group_kernel,
        [bf16_shape(HALF, width), bf16_shape(HALF, width), bf16_shape(HALF, CHUNK)],
        [pltpu.VMEM((GROUP, CHUNK), BF16)],
        8,
        place,
        lengths,
        got,
    )

    pair_tokens = jnp.concatenate([near_tokens, swap_core(given_tokens)], axis=1)
    sent = jnp.broadcast_to(pair_tokens[None], (N_DP,) + pair_tokens.shape)
    got = lax.all_to_all(sent, DP, 0, 0, tiled=True)
    all_tokens = jnp.transpose(got.reshape(N_DP, N_CHIP, PART, CHUNK), (1, 0, 2, 3))

    own_high, own_low = split_bf16(decor_matrix)
    far_high = swap_core(own_high)
    pair_matrix = jnp.concatenate([own_high, far_high], axis=1)
    partial_white = dot(all_tokens.reshape(ROWS // 2, CHUNK), pair_matrix, CONTRACT_LAST)

    got = lax.all_to_all(
        partial_white.astype(BF16).reshape(N_CHIP, HALF, CHUNK), CHIPS, 0, 0, tiled=True
    )
    white_chunk = jnp.sum(got.astype(F32), axis=0).astype(BF16).reshape(N_DP, PART, CHUNK)

    white_part = lax.all_to_all(white_chunk, DP, 0, 0, tiled=True)

    sent = jnp.concatenate(
        [white_part.reshape(HALF, CHUNK), white_chunk.reshape(HALF, CHUNK), cot_packed], axis=0
    )
    sent = jnp.broadcast_to(sent[None], (N_CHIP,) + sent.shape)
    got = lax.all_to_all(sent, CHIPS, 0, 0, tiled=True)

    def wide_rows(block):
        block = block.reshape(N_CHIP, N_DP, PART, CHUNK)
        return jnp.transpose(block, (0, 2, 1, 3)).reshape(HALF, N_DP * CHUNK)

    decor_near = wide_rows(got[:, HALF : 2 * HALF])
    cot_near = got[:, 2 * HALF :]
    feed_near = wide_rows(got[:, :HALF])
    decor_far = swap_core(decor_near)
    cot_far = swap_core(cot_near)
    feed_far = swap_core(feed_near)

    group_row = jnp.arange(GROUP, dtype=jnp.int32) * N_DP
    all_rows = (jnp.arange(N_DP, dtype=jnp.int32)[:, None] + group_row[None, :]).reshape(-1)
    row_weights = packed_weights(lengths, all_rows)
    own_weights = packed_weights(lengths, own_rank + group_row)
    white_rows, mixed_part = mixed_terms(core_list, decor_near, decor_far, own_high, own_low)
    white_rows = white_rows.reshape(ROWS, CHUNK)
    mixed_got = lax.all_to_all(mixed_part, DP, 0, 0, tiled=True)
    mixed_own = jnp.sum(mixed_got.astype(F32), axis=0)
    weighted_own = (mixed_own * own_weights[:, None]).astype(BF16)
    white_float = white_rows.astype(F32)
    diagonal = jnp.sum(row_weights[:, None] * white_float * white_float, axis=0)
    feed_near = lax.optimization_barrier((feed_near, mixed_part))[0]

    kept, given = feed_forward(
        core_list, feed_near, feed_far, cot_near, cot_far, in_weight, out_weight
    )
    given = lax.optimization_barrier((given, mixed_got))[0]
    summed = (kept.astype(F32) + swap_core(given).astype(F32)).astype(BF16)
    got = lax.all_to_all(summed, CHIPS, 0, 0, tiled=True)

    (sent,) = small_call(
        spread_kernel,
        [bf16_shape(N_DP, 2 * SLOTS + GROUP, width)],
        [pltpu.VMEM((2 * GROUP, width), BF16)],
        12,
        place,
        lengths,
        got,
        weighted_own,
    )
    got = lax.all_to_all(sent, DP, 0, 0, tiled=True)
    return tuple(
        small_call(
            final_kernel,
            [
                bf16_shape(*tokens.shape),
                bf16_shape(*tokens.shape),
                jax.ShapeDtypeStruct(decor_matrix.shape, F32),
            ],
            [],
            16,
            place,
            lengths,
            got,
            white_rows,
            diagonal[:, None],
            decor_matrix,
        )
    )


def solution(mesh):
    fine = Mesh(mesh.devices.reshape(4, 2, 2, 4, 2), ("x", "yl", "yh", "z", "core"))
    tensor = ("yh", "z", "core")
    placed = (
        P(DP, tensor),
        P(DP, tensor),
        P(DP, tensor),
        P(None, tensor),
        P(tensor, None),
        P(),
    )
    return jax.shard_map(
        local,
        mesh=fine,
        in_specs=placed,
        out_specs=(P(DP, tensor), P(DP, tensor), P(DP, tensor)),
        check_vma=False,
    )
```

```python
import math

import jax
import jax.numpy as jnp
from jax import lax
from jax.experimental import pallas as pl
from jax.experimental.pallas import tpu as pltpu
from jax.sharding import Mesh, PartitionSpec as P

GELU_SCALE = math.sqrt(2.0 / math.pi)
GELU_CUBIC = 0.044715
BF16 = jnp.bfloat16
F32 = jnp.float32
CONTRACT_LAST = (((1,), (1,)), ((), ()))
CONTRACT_FIRST = (((0,), (0,)), ((), ()))
DP = ("x", "yl")
CHIPS = ("yh", "z")
CORE = "core"
N_DP = 8
N_CHIP = 8
GROUP = 128
PART = 8
HALF = 64
ROWS = 1024
CHUNK = 768
SLOTS = 48
WEIGHT_COPIES = 4


def gelu_pair(values):
    inner_arg = GELU_SCALE * (values + GELU_CUBIC * values * values * values)
    tangent = jnp.tanh(inner_arg)
    output = 0.5 * values * (1.0 + tangent)
    gelu_slope = 0.5 * (1.0 + tangent) + 0.5 * values * (1.0 - tangent * tangent) * GELU_SCALE * (
        1.0 + 3.0 * GELU_CUBIC * values * values
    )
    return (output, gelu_slope)


def packed_weights(lengths, packed_index):
    flat_lengths = lengths.reshape(-1)
    seq_ends = jnp.cumsum(flat_lengths)
    seq_starts = seq_ends - flat_lengths
    member = (packed_index[:, None] >= seq_starts[None, :]) & (
        packed_index[:, None] < seq_ends[None, :]
    )
    seq_share = 1.0 / (lengths.shape[1] * flat_lengths.astype(F32))
    return jnp.sum(jnp.where(member, seq_share[None, :], 0.0), axis=1)


def split_bf16(values):
    high = lax.reduce_precision(values, 8, 7)
    return (high.astype(BF16), (values - high).astype(BF16))


def dot(left, right, numbers=(((1,), (0,)), ((), ()))):
    return lax.dot_general(left, right, numbers, preferred_element_type=F32)


def swap_core(value):
    return lax.ppermute(value, CORE, [(0, 1), (1, 0)])


def mixed_kernel(core_ref, near_ref, far_ref, high_ref, low_ref, rows_ref, mixed_ref):
    own = pl.multiple_of(core_ref[0] * HALF, HALF)
    other = pl.multiple_of(HALF - core_ref[0] * HALF, HALF)
    for group in range(N_DP):
        columns = pl.ds(group * CHUNK, CHUNK)
        rows_ref[group, pl.ds(own, HALF), :] = near_ref[:, columns]
        rows_ref[group, pl.ds(other, HALF), :] = far_ref[:, columns]
    rows = rows_ref[...].reshape(ROWS, CHUNK)
    total = dot(rows, high_ref[...]) + dot(rows, low_ref[...])
    mixed_ref[...] = total.astype(BF16).reshape(mixed_ref.shape)


def mixed_terms(core, near, far, high, low):
    vmem = pl.BlockSpec(memory_space=pltpu.VMEM)
    return pl.pallas_call(
        mixed_kernel,
        in_specs=[pl.BlockSpec(memory_space=pltpu.SMEM)] + [vmem] * 4,
        out_specs=[vmem, vmem],
        out_shape=[
            jax.ShapeDtypeStruct((N_DP, GROUP, CHUNK), BF16),
            jax.ShapeDtypeStruct((N_DP, GROUP, high.shape[1]), BF16),
        ],
        compiler_params=pltpu.CompilerParams(vmem_limit_bytes=16 << 20),
        cost_estimate=pl.CostEstimate(
            flops=4 * ROWS * CHUNK * 384, bytes_accessed=5 << 20, transcendentals=0
        ),
        name="mixed_terms",
    )(core, near, far, high, low)


def feed_kernel(
    core_ref, near_ref, far_ref, back_ref, in_ref, out_ref, kept_ref, given_ref,
    in_buf, out_buf, rows_buf, hidden_buf, delta_buf, in_sem, out_sem,
):
    own = pl.multiple_of(core_ref[0] * HALF, HALF)
    other = pl.multiple_of(HALF - core_ref[0] * HALF, HALF)
    first_core = core_ref[0] == 0
    steps = kept_ref.shape[0]
    width = CHUNK // 2
    in_copies, out_copies = [], []
    for step in range(WEIGHT_COPIES):
        rows = pl.ds(step * (in_buf.shape[0] // WEIGHT_COPIES), in_buf.shape[0] // WEIGHT_COPIES)
        in_copies.append(
            pltpu.make_async_copy(in_ref.at[rows, :], in_buf.at[rows, :], in_sem.at[step])
        )
        columns = pl.ds(
            step * (out_buf.shape[1] // WEIGHT_COPIES), out_buf.shape[1] // WEIGHT_COPIES
        )
        out_copies.append(
            pltpu.make_async_copy(out_ref.at[:, columns], out_buf.at[:, columns], out_sem.at[step])
        )
    for copy in in_copies + out_copies:
        copy.start()
    rows_buf[pl.ds(own, HALF), :] = near_ref[...]
    rows_buf[pl.ds(other, HALF), :] = far_ref[...]
    pre_act = 0.0
    depth = in_buf.shape[0] // WEIGHT_COPIES
    for step in range(WEIGHT_COPIES):
        span = pl.ds(step * depth, depth)
        in_copies[step].wait()
        pre_act = pre_act + dot(rows_buf[:, span], in_buf[span, :])
    gelu_out, gelu_slope = gelu_pair(pre_act)
    hidden_buf[...] = gelu_out.astype(BF16)
    delta_buf[...] = (back_ref[...] * gelu_slope).astype(BF16)

    def store(step, place, value):
        left, right = value[:, :width], value[:, width:]
        rows = pl.ds(place, GROUP)
        kept_ref[step, rows, :] = jnp.where(first_core, left, right).astype(BF16)
        given_ref[step, rows, :] = jnp.where(first_core, right, left).astype(BF16)

    for step in range(steps):
        columns = pl.ds(step * CHUNK, CHUNK)
        store(step, GROUP, dot(delta_buf[...], in_buf[columns, :], CONTRACT_LAST))
    for copy in out_copies:
        copy.wait()
    for step in range(steps):
        columns = pl.ds(step * CHUNK, CHUNK)
        store(step, 0, dot(hidden_buf[...], out_buf[:, columns]))


def feed_forward(core, near, far, back, in_weight, out_weight):
    vmem = pl.BlockSpec(memory_space=pltpu.VMEM)
    anywhere = pl.BlockSpec(memory_space=pl.ANY)
    steps = in_weight.shape[0] // CHUNK
    hidden = in_weight.shape[1]
    part = jax.ShapeDtypeStruct((steps, 2 * GROUP, CHUNK // 2), BF16)
    return pl.pallas_call(
        feed_kernel,
        in_specs=[pl.BlockSpec(memory_space=pltpu.SMEM)] + [vmem] * 3 + [anywhere] * 2,
        out_specs=[vmem, vmem],
        out_shape=[part, part],
        scratch_shapes=[
            pltpu.VMEM(in_weight.shape, BF16),
            pltpu.VMEM(out_weight.shape, BF16),
            pltpu.VMEM((GROUP, steps * CHUNK), BF16),
            pltpu.VMEM((GROUP, hidden), BF16),
            pltpu.VMEM((GROUP, hidden), BF16),
            pltpu.SemaphoreType.DMA((WEIGHT_COPIES,)),
            pltpu.SemaphoreType.DMA((WEIGHT_COPIES,)),
        ],
        compiler_params=pltpu.CompilerParams(vmem_limit_bytes=46 << 20),
        cost_estimate=pl.CostEstimate(flops=1 << 20, bytes_accessed=1 << 16, transcendentals=0),
        name="feed_forward",
    )(core, near, far, back, in_weight, out_weight)


def back_kernel(core_ref, near_ref, far_ref, out_ref, back_ref, out_buf, rows_buf, sem):
    first_core = core_ref[0] == 0
    width = CHUNK // 2
    copies = []
    for chip in range(N_CHIP):
        columns = pl.ds(chip * CHUNK, CHUNK)
        copies.append(
            pltpu.make_async_copy(out_ref.at[:, columns], out_buf.at[:, columns], sem.at[chip])
        )
        copies[-1].start()
    total = 0.0
    for chip in range(N_CHIP):
        columns = pl.ds(chip * CHUNK, CHUNK)
        for half in range(2):
            lanes = pl.ds(half * width, width)
            close, away = near_ref[chip, :, lanes], far_ref[chip, :, lanes]
            rows = pl.ds(half * HALF, HALF)
            rows_buf[rows, pl.ds(chip * CHUNK, width)] = jnp.where(first_core, close, away)
            rows_buf[rows, pl.ds(chip * CHUNK + width, width)] = jnp.where(first_core, away, close)
        copies[chip].wait()
        total = total + dot(rows_buf[:, columns], out_buf[:, columns], CONTRACT_LAST)
    back_ref[...] = total


def back_terms(core, near, far, out_weight):
    vmem = pl.BlockSpec(memory_space=pltpu.VMEM)
    hidden = out_weight.shape[0]
    return pl.pallas_call(
        back_kernel,
        in_specs=[pl.BlockSpec(memory_space=pltpu.SMEM), vmem, vmem]
        + [pl.BlockSpec(memory_space=pl.ANY)],
        out_specs=vmem,
        out_shape=jax.ShapeDtypeStruct((GROUP, hidden), F32),
        scratch_shapes=[
            pltpu.VMEM(out_weight.shape, BF16),
            pltpu.VMEM((GROUP, out_weight.shape[1]), BF16),
            pltpu.SemaphoreType.DMA((N_CHIP,)),
        ],
        compiler_params=pltpu.CompilerParams(vmem_limit_bytes=46 << 20),
        cost_estimate=pl.CostEstimate(flops=1 << 20, bytes_accessed=1 << 16, transcendentals=0),
        name="back_terms",
    )(core, near, far, out_weight)


def rank_spans(lengths_ref):
    live, starts, total = [], [], 0
    for rank in range(N_DP):
        count = lengths_ref[rank, 0]
        for column in range(1, lengths_ref.shape[1]):
            count = count + lengths_ref[rank, column]
        live.append(count)
        starts.append(total)
        total = total + count
    return live, starts


def entry_of(values, rank):
    found = values[0]
    for place in range(1, N_DP):
        found = jnp.where(rank == place, values[place], found)
    return found


def first_row(group, start):
    return lax.rem(group + ROWS - start, N_DP)


def one_hot(condition):
    return condition.astype(F32).astype(BF16)


def pack_kernel(place_ref, lengths_ref, tokens_ref, cot_ref, sent_ref):
    live, starts = rank_spans(lengths_ref)
    start, own_live = entry_of(starts, place_ref[0]), entry_of(live, place_ref[0])
    row_total, width = tokens_ref.shape
    slot = lax.broadcasted_iota(jnp.int32, (SLOTS, row_total), 0)
    row = lax.broadcasted_iota(jnp.int32, (SLOTS, row_total), 1)
    for group in range(N_DP):
        wanted = slot * N_DP + first_row(group, start)
        pick = one_hot((row == wanted) & (row < own_live))
        sent_ref[group, :, pl.ds(0, width)] = dot(pick, tokens_ref[...]).astype(BF16)
        sent_ref[group, :, pl.ds(width, width)] = dot(pick, cot_ref[...]).astype(BF16)


def group_kernel(place_ref, lengths_ref, got_ref, near_ref, given_ref, cot_ref, rows_buf):
    live, starts = rank_spans(lengths_ref)
    group, core = place_ref[0], place_ref[1]
    row = lax.broadcasted_iota(jnp.int32, (GROUP, SLOTS), 0)
    slot = lax.broadcasted_iota(jnp.int32, (GROUP, SLOTS), 1)
    total = jnp.zeros((GROUP, CHUNK), F32)
    for rank in range(N_DP):
        first = first_row(group, starts[rank])
        shift = (starts[rank] + first - group) // N_DP
        pick = one_hot((row == slot + shift) & (slot * N_DP + first < live[rank]))
        total = total + dot(pick, got_ref[rank])
    rows_buf[...] = total.astype(BF16)
    width = CHUNK // 2
    left, right = pl.ds(0, width), pl.ds(width, width)
    near_ref[...] = rows_buf[pl.ds(pl.multiple_of(core * HALF, HALF), HALF), left]
    given_ref[...] = rows_buf[pl.ds(pl.multiple_of(HALF - core * HALF, HALF), HALF), left]
    cot_ref[:, left] = rows_buf[pl.ds(0, HALF), right]
    cot_ref[:, right] = rows_buf[pl.ds(HALF, HALF), right]


def spread_kernel(place_ref, lengths_ref, got_ref, mixed_ref, sent_ref, rows_buf):
    live, starts = rank_spans(lengths_ref)
    group = place_ref[0]
    total = got_ref[0].astype(F32)
    for chip in range(1, N_CHIP):
        total = total + got_ref[chip].astype(F32)
    rows_buf[...] = total.astype(BF16)
    slot = lax.broadcasted_iota(jnp.int32, (SLOTS, GROUP), 0)
    row = lax.broadcasted_iota(jnp.int32, (SLOTS, GROUP), 1)
    for rank in range(N_DP):
        first = first_row(group, starts[rank])
        shift = (starts[rank] + first - group) // N_DP
        pick = one_hot((row == slot + shift) & (slot * N_DP + first < live[rank]))
        for half in range(2):
            rows = rows_buf[pl.ds(half * GROUP, GROUP), :]
            sent_ref[rank, pl.ds(half * SLOTS, SLOTS), :] = dot(pick, rows).astype(BF16)
        sent_ref[rank, pl.ds(2 * SLOTS, GROUP), :] = mixed_ref[...]


def final_kernel(
    place_ref, lengths_ref, got_ref, rows_ref, diagonal_ref, matrix_ref, out_ref, grad_ref, step_ref
):
    live, starts = rank_spans(lengths_ref)
    start, own_live = entry_of(starts, place_ref[0]), entry_of(live, place_ref[0])
    row_total, width = out_ref.shape
    row = lax.broadcasted_iota(jnp.int32, (row_total, SLOTS), 0)
    slot = lax.broadcasted_iota(jnp.int32, (row_total, SLOTS), 1)
    out_total = jnp.zeros((row_total, width), F32)
    grad_total = jnp.zeros((row_total, width), F32)
    for group in range(N_DP):
        wanted = slot * N_DP + first_row(group, start)
        pick = one_hot((row == wanted) & (row < own_live))
        out_total = out_total + dot(pick, got_ref[group, pl.ds(0, SLOTS), :])
        grad_total = grad_total + dot(pick, got_ref[group, pl.ds(SLOTS, SLOTS), :])
    out_ref[...] = out_total.astype(BF16)
    grad_ref[...] = grad_total.astype(BF16)
    mixed = got_ref[:, pl.ds(2 * SLOTS, GROUP), :].reshape(ROWS, width)
    product = dot(rows_ref[...], mixed, CONTRACT_FIRST)
    step_ref[...] = product - diagonal_ref[...] * matrix_ref[...]


def small_call(kernel, shapes, scratch, limit, *operands):
    smem = pl.BlockSpec(memory_space=pltpu.SMEM)
    vmem = pl.BlockSpec(memory_space=pltpu.VMEM)
    return pl.pallas_call(
        kernel,
        in_specs=[smem, smem] + [vmem] * (len(operands) - 2),
        out_specs=[vmem] * len(shapes),
        out_shape=shapes,
        scratch_shapes=scratch,
        compiler_params=pltpu.CompilerParams(vmem_limit_bytes=limit << 20),
        cost_estimate=pl.CostEstimate(flops=1 << 20, bytes_accessed=1 << 16, transcendentals=0),
        name=kernel.__name__,
    )(*operands)


def local(tokens, cotangent, decor_matrix, in_weight, out_weight, lengths):
    width = tokens.shape[1]
    own_rank = lax.axis_index(DP)
    core = lax.axis_index(CORE)
    core_list = core.reshape(1)
    place = jnp.stack([own_rank, core])

    def bf16_shape(*shape):
        return jax.ShapeDtypeStruct(shape, BF16)

    (sent,) = small_call(
        pack_kernel, [bf16_shape(N_DP, SLOTS, CHUNK)], [], 8, place, lengths, tokens, cotangent
    )
    got = lax.all_to_all(sent, DP, 0, 0, tiled=True)
    near_tokens, given_tokens, cot_packed = small_call(
        group_kernel,
        [bf16_shape(HALF, width), bf16_shape(HALF, width), bf16_shape(HALF, CHUNK)],
        [pltpu.VMEM((GROUP, CHUNK), BF16)],
        8,
        place,
        lengths,
        got,
    )

    pair_tokens = jnp.concatenate([near_tokens, swap_core(given_tokens)], axis=1)
    sent = jnp.broadcast_to(pair_tokens[None], (N_DP,) + pair_tokens.shape)
    got = lax.all_to_all(sent, DP, 0, 0, tiled=True)
    all_tokens = jnp.transpose(got.reshape(N_DP, N_CHIP, PART, CHUNK), (1, 0, 2, 3))

    own_high, own_low = split_bf16(decor_matrix)
    far_high = swap_core(own_high)
    pair_matrix = jnp.concatenate([own_high, far_high], axis=1)
    partial_white = dot(all_tokens.reshape(ROWS // 2, CHUNK), pair_matrix, CONTRACT_LAST)

    sent = jnp.concatenate(
        [
            partial_white.astype(BF16).reshape(N_CHIP, HALF, CHUNK),
            jnp.broadcast_to(cot_packed[None], (N_CHIP,) + cot_packed.shape),
        ],
        axis=1,
    )
    got = lax.all_to_all(sent, CHIPS, 0, 0, tiled=True)
    cot_near = got[:, HALF:]
    back_hidden = back_terms(core_list, cot_near, swap_core(cot_near), out_weight)
    white_chunk = jnp.sum(got[:, :HALF].astype(F32), axis=0).astype(BF16).reshape(N_DP, PART, CHUNK)

    white_part = lax.all_to_all(white_chunk, DP, 0, 0, tiled=True)

    sent = jnp.concatenate(
        [white_part.reshape(HALF, CHUNK), white_chunk.reshape(HALF, CHUNK)], axis=0
    )
    sent = jnp.broadcast_to(sent[None], (N_CHIP,) + sent.shape)
    got = lax.all_to_all(sent, CHIPS, 0, 0, tiled=True)

    got = lax.optimization_barrier((got, back_hidden))[0]

    def wide_rows(block):
        block = block.reshape(N_CHIP, N_DP, PART, CHUNK)
        return jnp.transpose(block, (0, 2, 1, 3)).reshape(HALF, N_DP * CHUNK)

    decor_near = wide_rows(got[:, HALF:])
    feed_near = wide_rows(got[:, :HALF])
    decor_far = swap_core(decor_near)
    feed_far = swap_core(feed_near)

    group_row = jnp.arange(GROUP, dtype=jnp.int32) * N_DP
    all_rows = (jnp.arange(N_DP, dtype=jnp.int32)[:, None] + group_row[None, :]).reshape(-1)
    row_weights = packed_weights(lengths, all_rows)
    own_weights = packed_weights(lengths, own_rank + group_row)
    white_rows, mixed_part = mixed_terms(core_list, decor_near, decor_far, own_high, own_low)
    white_rows = white_rows.reshape(ROWS, CHUNK)
    mixed_got = lax.all_to_all(mixed_part, DP, 0, 0, tiled=True)
    mixed_own = jnp.sum(mixed_got.astype(F32), axis=0)
    weighted_own = (mixed_own * own_weights[:, None]).astype(BF16)
    white_float = white_rows.astype(F32)
    diagonal = jnp.sum(row_weights[:, None] * white_float * white_float, axis=0)
    feed_near = lax.optimization_barrier((feed_near, mixed_part))[0]

    kept, given = feed_forward(
        core_list, feed_near, feed_far, back_hidden, in_weight, out_weight
    )
    given = lax.optimization_barrier((given, mixed_got))[0]
    summed = (kept.astype(F32) + swap_core(given).astype(F32)).astype(BF16)
    got = lax.all_to_all(summed, CHIPS, 0, 0, tiled=True)

    (sent,) = small_call(
        spread_kernel,
        [bf16_shape(N_DP, 2 * SLOTS + GROUP, width)],
        [pltpu.VMEM((2 * GROUP, width), BF16)],
        12,
        place,
        lengths,
        got,
        weighted_own,
    )
    got = lax.all_to_all(sent, DP, 0, 0, tiled=True)
    return tuple(
        small_call(
            final_kernel,
            [
                bf16_shape(*tokens.shape),
                bf16_shape(*tokens.shape),
                jax.ShapeDtypeStruct(decor_matrix.shape, F32),
            ],
            [],
            16,
            place,
            lengths,
            got,
            white_rows,
            diagonal[:, None],
            decor_matrix,
        )
    )


def solution(mesh):
    fine = Mesh(mesh.devices.reshape(4, 2, 2, 4, 2), ("x", "yl", "yh", "z", "core"))
    tensor = ("yh", "z", "core")
    placed = (
        P(DP, tensor),
        P(DP, tensor),
        P(DP, tensor),
        P(None, tensor),
        P(tensor, None),
        P(),
    )
    return jax.shard_map(
        local,
        mesh=fine,
        in_specs=placed,
        out_specs=(P(DP, tensor), P(DP, tensor), P(DP, tensor)),
        check_vma=False,
    )
```

```python
import math

import jax
import jax.numpy as jnp
from jax import lax
from jax.experimental import pallas as pl
from jax.experimental.pallas import tpu as pltpu
from jax.sharding import Mesh, PartitionSpec as P

GELU_SCALE = math.sqrt(2.0 / math.pi)
GELU_CUBIC = 0.044715
BF16 = jnp.bfloat16
F32 = jnp.float32
CONTRACT_LAST = (((1,), (1,)), ((), ()))
CONTRACT_FIRST = (((0,), (0,)), ((), ()))
DP = ("x", "yl")
CHIPS = ("yh", "z")
CORE = "core"
N_DP = 8
N_CHIP = 8
GROUP = 128
PART = 8
HALF = 64
ROWS = 1024
CHUNK = 768
SLOTS = 48
WEIGHT_COPIES = 4


def gelu_pair(values):
    inner_arg = GELU_SCALE * (values + GELU_CUBIC * values * values * values)
    tangent = jnp.tanh(inner_arg)
    output = 0.5 * values * (1.0 + tangent)
    gelu_slope = 0.5 * (1.0 + tangent) + 0.5 * values * (1.0 - tangent * tangent) * GELU_SCALE * (
        1.0 + 3.0 * GELU_CUBIC * values * values
    )
    return (output, gelu_slope)


def packed_weights(lengths, packed_index):
    flat_lengths = lengths.reshape(-1)
    seq_ends = jnp.cumsum(flat_lengths)
    seq_starts = seq_ends - flat_lengths
    member = (packed_index[:, None] >= seq_starts[None, :]) & (
        packed_index[:, None] < seq_ends[None, :]
    )
    seq_share = 1.0 / (lengths.shape[1] * flat_lengths.astype(F32))
    return jnp.sum(jnp.where(member, seq_share[None, :], 0.0), axis=1)


def split_bf16(values):
    high = lax.reduce_precision(values, 8, 7)
    return (high.astype(BF16), (values - high).astype(BF16))


def dot(left, right, numbers=(((1,), (0,)), ((), ()))):
    return lax.dot_general(left, right, numbers, preferred_element_type=F32)


def swap_core(value):
    return lax.ppermute(value, CORE, [(0, 1), (1, 0)])


def mixed_kernel(core_ref, near_ref, far_ref, high_ref, low_ref, rows_ref, mixed_ref):
    own = pl.multiple_of(core_ref[0] * HALF, HALF)
    other = pl.multiple_of(HALF - core_ref[0] * HALF, HALF)
    for group in range(N_DP):
        columns = pl.ds(group * CHUNK, CHUNK)
        rows_ref[group, pl.ds(own, HALF), :] = near_ref[:, columns]
        rows_ref[group, pl.ds(other, HALF), :] = far_ref[:, columns]
    rows = rows_ref[...].reshape(ROWS, CHUNK)
    total = dot(rows, high_ref[...]) + dot(rows, low_ref[...])
    mixed_ref[...] = total.astype(BF16).reshape(mixed_ref.shape)


def mixed_terms(core, near, far, high, low):
    vmem = pl.BlockSpec(memory_space=pltpu.VMEM)
    return pl.pallas_call(
        mixed_kernel,
        in_specs=[pl.BlockSpec(memory_space=pltpu.SMEM)] + [vmem] * 4,
        out_specs=[vmem, vmem],
        out_shape=[
            jax.ShapeDtypeStruct((N_DP, GROUP, CHUNK), BF16),
            jax.ShapeDtypeStruct((N_DP, GROUP, high.shape[1]), BF16),
        ],
        compiler_params=pltpu.CompilerParams(vmem_limit_bytes=16 << 20),
        cost_estimate=pl.CostEstimate(
            flops=4 * ROWS * CHUNK * 384, bytes_accessed=5 << 20, transcendentals=0
        ),
        name="mixed_terms",
    )(core, near, far, high, low)


def feed_kernel(
    core_ref, near_ref, far_ref, back_ref, in_ref, out_ref, kept_ref, given_ref,
    in_buf, out_buf, rows_buf, hidden_buf, delta_buf, in_sem, out_sem,
):
    own = pl.multiple_of(core_ref[0] * HALF, HALF)
    other = pl.multiple_of(HALF - core_ref[0] * HALF, HALF)
    first_core = core_ref[0] == 0
    steps = kept_ref.shape[0]
    width = CHUNK // 2
    in_copies, out_copies = [], []
    for step in range(WEIGHT_COPIES):
        rows = pl.ds(step * (in_buf.shape[0] // WEIGHT_COPIES), in_buf.shape[0] // WEIGHT_COPIES)
        in_copies.append(
            pltpu.make_async_copy(in_ref.at[rows, :], in_buf.at[rows, :], in_sem.at[step])
        )
        columns = pl.ds(
            step * (out_buf.shape[1] // WEIGHT_COPIES), out_buf.shape[1] // WEIGHT_COPIES
        )
        out_copies.append(
            pltpu.make_async_copy(out_ref.at[:, columns], out_buf.at[:, columns], out_sem.at[step])
        )
    for copy in in_copies:
        copy.start()
    rows_buf[pl.ds(own, HALF), :] = near_ref[...]
    rows_buf[pl.ds(other, HALF), :] = far_ref[...]
    pre_act = 0.0
    depth = in_buf.shape[0] // WEIGHT_COPIES
    for step in range(WEIGHT_COPIES):
        span = pl.ds(step * depth, depth)
        in_copies[step].wait()
        out_copies[step].start()
        pre_act = pre_act + dot(rows_buf[:, span], in_buf[span, :])
    gelu_out, gelu_slope = gelu_pair(pre_act)
    hidden_buf[...] = gelu_out.astype(BF16)
    delta_buf[...] = (back_ref[...] * gelu_slope).astype(BF16)

    def store(step, place, value):
        left, right = value[:, :width], value[:, width:]
        rows = pl.ds(place, GROUP)
        kept_ref[step, rows, :] = jnp.where(first_core, left, right).astype(BF16)
        given_ref[step, rows, :] = jnp.where(first_core, right, left).astype(BF16)

    for step in range(steps):
        columns = pl.ds(step * CHUNK, CHUNK)
        store(step, GROUP, dot(delta_buf[...], in_buf[columns, :], CONTRACT_LAST))
    for copy in out_copies:
        copy.wait()
    for step in range(steps):
        columns = pl.ds(step * CHUNK, CHUNK)
        store(step, 0, dot(hidden_buf[...], out_buf[:, columns]))


def feed_forward(core, near, far, back, in_weight, out_weight):
    vmem = pl.BlockSpec(memory_space=pltpu.VMEM)
    anywhere = pl.BlockSpec(memory_space=pl.ANY)
    steps = in_weight.shape[0] // CHUNK
    hidden = in_weight.shape[1]
    part = jax.ShapeDtypeStruct((steps, 2 * GROUP, CHUNK // 2), BF16)
    return pl.pallas_call(
        feed_kernel,
        in_specs=[pl.BlockSpec(memory_space=pltpu.SMEM)] + [vmem] * 3 + [anywhere] * 2,
        out_specs=[vmem, vmem],
        out_shape=[part, part],
        scratch_shapes=[
            pltpu.VMEM(in_weight.shape, BF16),
            pltpu.VMEM(out_weight.shape, BF16),
            pltpu.VMEM((GROUP, steps * CHUNK), BF16),
            pltpu.VMEM((GROUP, hidden), BF16),
            pltpu.VMEM((GROUP, hidden), BF16),
            pltpu.SemaphoreType.DMA((WEIGHT_COPIES,)),
            pltpu.SemaphoreType.DMA((WEIGHT_COPIES,)),
        ],
        compiler_params=pltpu.CompilerParams(vmem_limit_bytes=46 << 20),
        cost_estimate=pl.CostEstimate(flops=1 << 20, bytes_accessed=1 << 16, transcendentals=0),
        name="feed_forward",
    )(core, near, far, back, in_weight, out_weight)


def back_kernel(core_ref, near_ref, far_ref, out_ref, back_ref, out_buf, rows_buf, sem):
    first_core = core_ref[0] == 0
    width = CHUNK // 2
    copies = []
    for chip in range(N_CHIP):
        columns = pl.ds(chip * CHUNK, CHUNK)
        copies.append(
            pltpu.make_async_copy(out_ref.at[:, columns], out_buf.at[:, columns], sem.at[chip])
        )
        copies[-1].start()
    total = 0.0
    for chip in range(N_CHIP):
        columns = pl.ds(chip * CHUNK, CHUNK)
        for half in range(2):
            lanes = pl.ds(half * width, width)
            close, away = near_ref[chip, :, lanes], far_ref[chip, :, lanes]
            rows = pl.ds(half * HALF, HALF)
            rows_buf[rows, pl.ds(chip * CHUNK, width)] = jnp.where(first_core, close, away)
            rows_buf[rows, pl.ds(chip * CHUNK + width, width)] = jnp.where(first_core, away, close)
        copies[chip].wait()
        total = total + dot(rows_buf[:, columns], out_buf[:, columns], CONTRACT_LAST)
    back_ref[...] = total


def back_terms(core, near, far, out_weight):
    vmem = pl.BlockSpec(memory_space=pltpu.VMEM)
    hidden = out_weight.shape[0]
    return pl.pallas_call(
        back_kernel,
        in_specs=[pl.BlockSpec(memory_space=pltpu.SMEM), vmem, vmem]
        + [pl.BlockSpec(memory_space=pl.ANY)],
        out_specs=vmem,
        out_shape=jax.ShapeDtypeStruct((GROUP, hidden), F32),
        scratch_shapes=[
            pltpu.VMEM(out_weight.shape, BF16),
            pltpu.VMEM((GROUP, out_weight.shape[1]), BF16),
            pltpu.SemaphoreType.DMA((N_CHIP,)),
        ],
        compiler_params=pltpu.CompilerParams(vmem_limit_bytes=46 << 20),
        cost_estimate=pl.CostEstimate(flops=1 << 20, bytes_accessed=1 << 16, transcendentals=0),
        name="back_terms",
    )(core, near, far, out_weight)


def rank_spans(lengths_ref):
    live, starts, total = [], [], 0
    for rank in range(N_DP):
        count = lengths_ref[rank, 0]
        for column in range(1, lengths_ref.shape[1]):
            count = count + lengths_ref[rank, column]
        live.append(count)
        starts.append(total)
        total = total + count
    return live, starts


def entry_of(values, rank):
    found = values[0]
    for place in range(1, N_DP):
        found = jnp.where(rank == place, values[place], found)
    return found


def first_row(group, start):
    return lax.rem(group + ROWS - start, N_DP)


def one_hot(condition):
    return condition.astype(F32).astype(BF16)


def pack_kernel(place_ref, lengths_ref, tokens_ref, cot_ref, sent_ref):
    live, starts = rank_spans(lengths_ref)
    start, own_live = entry_of(starts, place_ref[0]), entry_of(live, place_ref[0])
    row_total, width = tokens_ref.shape
    slot = lax.broadcasted_iota(jnp.int32, (SLOTS, row_total), 0)
    row = lax.broadcasted_iota(jnp.int32, (SLOTS, row_total), 1)
    for group in range(N_DP):
        wanted = slot * N_DP + first_row(group, start)
        pick = one_hot((row == wanted) & (row < own_live))
        sent_ref[group, :, pl.ds(0, width)] = dot(pick, tokens_ref[...]).astype(BF16)
        sent_ref[group, :, pl.ds(width, width)] = dot(pick, cot_ref[...]).astype(BF16)


def group_kernel(place_ref, lengths_ref, got_ref, near_ref, given_ref, cot_ref, rows_buf):
    live, starts = rank_spans(lengths_ref)
    group, core = place_ref[0], place_ref[1]
    row = lax.broadcasted_iota(jnp.int32, (GROUP, SLOTS), 0)
    slot = lax.broadcasted_iota(jnp.int32, (GROUP, SLOTS), 1)
    total = jnp.zeros((GROUP, CHUNK), F32)
    for rank in range(N_DP):
        first = first_row(group, starts[rank])
        shift = (starts[rank] + first - group) // N_DP
        pick = one_hot((row == slot + shift) & (slot * N_DP + first < live[rank]))
        total = total + dot(pick, got_ref[rank])
    rows_buf[...] = total.astype(BF16)
    width = CHUNK // 2
    left, right = pl.ds(0, width), pl.ds(width, width)
    near_ref[...] = rows_buf[pl.ds(pl.multiple_of(core * HALF, HALF), HALF), left]
    given_ref[...] = rows_buf[pl.ds(pl.multiple_of(HALF - core * HALF, HALF), HALF), left]
    cot_ref[:, left] = rows_buf[pl.ds(0, HALF), right]
    cot_ref[:, right] = rows_buf[pl.ds(HALF, HALF), right]


def spread_kernel(place_ref, lengths_ref, got_ref, mixed_ref, sent_ref, rows_buf):
    live, starts = rank_spans(lengths_ref)
    group = place_ref[0]
    total = got_ref[0].astype(F32)
    for chip in range(1, N_CHIP):
        total = total + got_ref[chip].astype(F32)
    rows_buf[...] = total.astype(BF16)
    slot = lax.broadcasted_iota(jnp.int32, (SLOTS, GROUP), 0)
    row = lax.broadcasted_iota(jnp.int32, (SLOTS, GROUP), 1)
    for rank in range(N_DP):
        first = first_row(group, starts[rank])
        shift = (starts[rank] + first - group) // N_DP
        pick = one_hot((row == slot + shift) & (slot * N_DP + first < live[rank]))
        for half in range(2):
            rows = rows_buf[pl.ds(half * GROUP, GROUP), :]
            sent_ref[rank, pl.ds(half * SLOTS, SLOTS), :] = dot(pick, rows).astype(BF16)
        sent_ref[rank, pl.ds(2 * SLOTS, GROUP), :] = mixed_ref[...]


def final_kernel(
    place_ref, lengths_ref, got_ref, rows_ref, diagonal_ref, matrix_ref, out_ref, grad_ref, step_ref
):
    live, starts = rank_spans(lengths_ref)
    start, own_live = entry_of(starts, place_ref[0]), entry_of(live, place_ref[0])
    row_total, width = out_ref.shape
    row = lax.broadcasted_iota(jnp.int32, (row_total, SLOTS), 0)
    slot = lax.broadcasted_iota(jnp.int32, (row_total, SLOTS), 1)
    out_total = jnp.zeros((row_total, width), F32)
    grad_total = jnp.zeros((row_total, width), F32)
    for group in range(N_DP):
        wanted = slot * N_DP + first_row(group, start)
        pick = one_hot((row == wanted) & (row < own_live))
        out_total = out_total + dot(pick, got_ref[group, pl.ds(0, SLOTS), :])
        grad_total = grad_total + dot(pick, got_ref[group, pl.ds(SLOTS, SLOTS), :])
    out_ref[...] = out_total.astype(BF16)
    grad_ref[...] = grad_total.astype(BF16)
    mixed = got_ref[:, pl.ds(2 * SLOTS, GROUP), :].reshape(ROWS, width)
    product = dot(rows_ref[...], mixed, CONTRACT_FIRST)
    step_ref[...] = product - diagonal_ref[...] * matrix_ref[...]


def small_call(kernel, shapes, scratch, limit, *operands):
    smem = pl.BlockSpec(memory_space=pltpu.SMEM)
    vmem = pl.BlockSpec(memory_space=pltpu.VMEM)
    return pl.pallas_call(
        kernel,
        in_specs=[smem, smem] + [vmem] * (len(operands) - 2),
        out_specs=[vmem] * len(shapes),
        out_shape=shapes,
        scratch_shapes=scratch,
        compiler_params=pltpu.CompilerParams(vmem_limit_bytes=limit << 20),
        cost_estimate=pl.CostEstimate(flops=1 << 20, bytes_accessed=1 << 16, transcendentals=0),
        name=kernel.__name__,
    )(*operands)


def local(tokens, cotangent, decor_matrix, in_weight, out_weight, lengths):
    width = tokens.shape[1]
    own_rank = lax.axis_index(DP)
    core = lax.axis_index(CORE)
    core_list = core.reshape(1)
    place = jnp.stack([own_rank, core])

    def bf16_shape(*shape):
        return jax.ShapeDtypeStruct(shape, BF16)

    (sent,) = small_call(
        pack_kernel, [bf16_shape(N_DP, SLOTS, CHUNK)], [], 8, place, lengths, tokens, cotangent
    )
    got = lax.all_to_all(sent, DP, 0, 0, tiled=True)
    near_tokens, given_tokens, cot_packed = small_call(
        group_kernel,
        [bf16_shape(HALF, width), bf16_shape(HALF, width), bf16_shape(HALF, CHUNK)],
        [pltpu.VMEM((GROUP, CHUNK), BF16)],
        8,
        place,
        lengths,
        got,
    )

    pair_tokens = jnp.concatenate([near_tokens, swap_core(given_tokens)], axis=1)
    sent = jnp.broadcast_to(pair_tokens[None], (N_DP,) + pair_tokens.shape)
    got = lax.all_to_all(sent, DP, 0, 0, tiled=True)
    all_tokens = jnp.transpose(got.reshape(N_DP, N_CHIP, PART, CHUNK), (1, 0, 2, 3))

    own_high, own_low = split_bf16(decor_matrix)
    far_high = swap_core(own_high)
    pair_matrix = jnp.concatenate([own_high, far_high], axis=1)
    partial_white = dot(all_tokens.reshape(ROWS // 2, CHUNK), pair_matrix, CONTRACT_LAST)

    sent = jnp.concatenate(
        [
            partial_white.astype(BF16).reshape(N_CHIP, HALF, CHUNK),
            jnp.broadcast_to(cot_packed[None], (N_CHIP,) + cot_packed.shape),
        ],
        axis=1,
    )
    got = lax.all_to_all(sent, CHIPS, 0, 0, tiled=True)
    cot_near = got[:, HALF:]
    back_hidden = back_terms(core_list, cot_near, swap_core(cot_near), out_weight)
    white_chunk = jnp.sum(got[:, :HALF].astype(F32), axis=0).astype(BF16).reshape(N_DP, PART, CHUNK)

    white_part = lax.all_to_all(white_chunk, DP, 0, 0, tiled=True)

    sent = jnp.concatenate(
        [white_part.reshape(HALF, CHUNK), white_chunk.reshape(HALF, CHUNK)], axis=0
    )
    sent = jnp.broadcast_to(sent[None], (N_CHIP,) + sent.shape)
    got = lax.all_to_all(sent, CHIPS, 0, 0, tiled=True)

    got = lax.optimization_barrier((got, back_hidden))[0]

    def wide_rows(block):
        block = block.reshape(N_CHIP, N_DP, PART, CHUNK)
        return jnp.transpose(block, (0, 2, 1, 3)).reshape(HALF, N_DP * CHUNK)

    decor_near = wide_rows(got[:, HALF:])
    feed_near = wide_rows(got[:, :HALF])
    decor_far = swap_core(decor_near)
    feed_far = swap_core(feed_near)

    group_row = jnp.arange(GROUP, dtype=jnp.int32) * N_DP
    all_rows = (jnp.arange(N_DP, dtype=jnp.int32)[:, None] + group_row[None, :]).reshape(-1)
    row_weights = packed_weights(lengths, all_rows)
    own_weights = packed_weights(lengths, own_rank + group_row)
    white_rows, mixed_part = mixed_terms(core_list, decor_near, decor_far, own_high, own_low)
    white_rows = white_rows.reshape(ROWS, CHUNK)
    mixed_got = lax.all_to_all(mixed_part, DP, 0, 0, tiled=True)
    mixed_own = jnp.sum(mixed_got.astype(F32), axis=0)
    weighted_own = (mixed_own * own_weights[:, None]).astype(BF16)
    white_float = white_rows.astype(F32)
    diagonal = jnp.sum(row_weights[:, None] * white_float * white_float, axis=0)
    feed_near = lax.optimization_barrier((feed_near, mixed_part))[0]

    kept, given = feed_forward(
        core_list, feed_near, feed_far, back_hidden, in_weight, out_weight
    )
    given = lax.optimization_barrier((given, mixed_got))[0]
    summed = (kept.astype(F32) + swap_core(given).astype(F32)).astype(BF16)
    got = lax.all_to_all(summed, CHIPS, 0, 0, tiled=True)

    (sent,) = small_call(
        spread_kernel,
        [bf16_shape(N_DP, 2 * SLOTS + GROUP, width)],
        [pltpu.VMEM((2 * GROUP, width), BF16)],
        12,
        place,
        lengths,
        got,
        weighted_own,
    )
    got = lax.all_to_all(sent, DP, 0, 0, tiled=True)
    return tuple(
        small_call(
            final_kernel,
            [
                bf16_shape(*tokens.shape),
                bf16_shape(*tokens.shape),
                jax.ShapeDtypeStruct(decor_matrix.shape, F32),
            ],
            [],
            16,
            place,
            lengths,
            got,
            white_rows,
            diagonal[:, None],
            decor_matrix,
        )
    )


def solution(mesh):
    fine = Mesh(mesh.devices.reshape(4, 2, 2, 4, 2), ("x", "yl", "yh", "z", "core"))
    tensor = ("yh", "z", "core")
    placed = (
        P(DP, tensor),
        P(DP, tensor),
        P(DP, tensor),
        P(None, tensor),
        P(tensor, None),
        P(),
    )
    return jax.shard_map(
        local,
        mesh=fine,
        in_specs=placed,
        out_specs=(P(DP, tensor), P(DP, tensor), P(DP, tensor)),
        check_vma=False,
    )
```

```python
import math

import jax
import jax.numpy as jnp
from jax import lax
from jax.experimental import pallas as pl
from jax.experimental.pallas import tpu as pltpu
from jax.sharding import Mesh, PartitionSpec as P

GELU_SCALE = math.sqrt(2.0 / math.pi)
GELU_CUBIC = 0.044715
BF16 = jnp.bfloat16
F32 = jnp.float32
CONTRACT_LAST = (((1,), (1,)), ((), ()))
CONTRACT_FIRST = (((0,), (0,)), ((), ()))
DP = ("x", "yl")
CHIPS = ("yh", "z")
CORE = "core"
N_DP = 8
N_CHIP = 8
GROUP = 128
PART = 8
HALF = 64
ROWS = 1024
CHUNK = 768
SLOTS = 48
WEIGHT_COPIES = 4


def gelu_pair(values):
    inner_arg = GELU_SCALE * (values + GELU_CUBIC * values * values * values)
    tangent = jnp.tanh(inner_arg)
    output = 0.5 * values * (1.0 + tangent)
    gelu_slope = 0.5 * (1.0 + tangent) + 0.5 * values * (1.0 - tangent * tangent) * GELU_SCALE * (
        1.0 + 3.0 * GELU_CUBIC * values * values
    )
    return (output, gelu_slope)


def packed_weights(lengths, packed_index):
    flat_lengths = lengths.reshape(-1)
    seq_ends = jnp.cumsum(flat_lengths)
    seq_starts = seq_ends - flat_lengths
    member = (packed_index[:, None] >= seq_starts[None, :]) & (
        packed_index[:, None] < seq_ends[None, :]
    )
    seq_share = 1.0 / (lengths.shape[1] * flat_lengths.astype(F32))
    return jnp.sum(jnp.where(member, seq_share[None, :], 0.0), axis=1)


def split_bf16(values):
    high = lax.reduce_precision(values, 8, 7)
    return (high.astype(BF16), (values - high).astype(BF16))


def dot(left, right, numbers=(((1,), (0,)), ((), ()))):
    return lax.dot_general(left, right, numbers, preferred_element_type=F32)


def swap_core(value):
    return lax.ppermute(value, CORE, [(0, 1), (1, 0)])


def mixed_kernel(core_ref, near_ref, far_ref, high_ref, low_ref, rows_ref, mixed_ref):
    own = pl.multiple_of(core_ref[0] * HALF, HALF)
    other = pl.multiple_of(HALF - core_ref[0] * HALF, HALF)
    for group in range(N_DP):
        columns = pl.ds(group * CHUNK, CHUNK)
        rows_ref[group, pl.ds(own, HALF), :] = near_ref[:, columns]
        rows_ref[group, pl.ds(other, HALF), :] = far_ref[:, columns]
    rows = rows_ref[...].reshape(ROWS, CHUNK)
    total = dot(rows, high_ref[...]) + dot(rows, low_ref[...])
    mixed_ref[...] = total.astype(BF16).reshape(mixed_ref.shape)


def mixed_terms(core, near, far, high, low):
    vmem = pl.BlockSpec(memory_space=pltpu.VMEM)
    return pl.pallas_call(
        mixed_kernel,
        in_specs=[pl.BlockSpec(memory_space=pltpu.SMEM)] + [vmem] * 4,
        out_specs=[vmem, vmem],
        out_shape=[
            jax.ShapeDtypeStruct((N_DP, GROUP, CHUNK), BF16),
            jax.ShapeDtypeStruct((N_DP, GROUP, high.shape[1]), BF16),
        ],
        compiler_params=pltpu.CompilerParams(vmem_limit_bytes=16 << 20),
        cost_estimate=pl.CostEstimate(
            flops=4 * ROWS * CHUNK * 384, bytes_accessed=5 << 20, transcendentals=0
        ),
        name="mixed_terms",
    )(core, near, far, high, low)


def feed_kernel(
    core_ref, near_ref, far_ref, back_ref, in_ref, out_ref, kept_ref, given_ref,
    in_buf, out_buf, rows_buf, hidden_buf, delta_buf, in_sem, out_sem,
):
    own = pl.multiple_of(core_ref[0] * HALF, HALF)
    other = pl.multiple_of(HALF - core_ref[0] * HALF, HALF)
    first_core = core_ref[0] == 0
    steps = kept_ref.shape[0]
    width = CHUNK // 2
    in_copies, out_copies = [], []
    for step in range(WEIGHT_COPIES):
        rows = pl.ds(step * (in_buf.shape[0] // WEIGHT_COPIES), in_buf.shape[0] // WEIGHT_COPIES)
        in_copies.append(
            pltpu.make_async_copy(in_ref.at[rows, :], in_buf.at[rows, :], in_sem.at[step])
        )
        columns = pl.ds(
            step * (out_buf.shape[1] // WEIGHT_COPIES), out_buf.shape[1] // WEIGHT_COPIES
        )
        out_copies.append(
            pltpu.make_async_copy(out_ref.at[:, columns], out_buf.at[:, columns], out_sem.at[step])
        )
    for copy in in_copies:
        copy.start()
    rows_buf[pl.ds(own, HALF), :] = near_ref[...]
    rows_buf[pl.ds(other, HALF), :] = far_ref[...]
    pre_act = 0.0
    depth = in_buf.shape[0] // WEIGHT_COPIES
    for step in range(WEIGHT_COPIES):
        span = pl.ds(step * depth, depth)
        in_copies[step].wait()
        out_copies[step].start()
        pre_act = pre_act + dot(rows_buf[:, span], in_buf[span, :])
    gelu_out, gelu_slope = gelu_pair(pre_act)
    hidden_buf[...] = gelu_out.astype(BF16)
    delta_buf[...] = (back_ref[...] * gelu_slope).astype(BF16)

    def store(step, place, value):
        left, right = value[:, :width], value[:, width:]
        rows = pl.ds(place, GROUP)
        kept_ref[step, rows, :] = jnp.where(first_core, left, right).astype(BF16)
        given_ref[step, rows, :] = jnp.where(first_core, right, left).astype(BF16)

    for step in range(steps):
        columns = pl.ds(step * CHUNK, CHUNK)
        store(step, GROUP, dot(delta_buf[...], in_buf[columns, :], CONTRACT_LAST))
    for copy in out_copies:
        copy.wait()
    for step in range(steps):
        columns = pl.ds(step * CHUNK, CHUNK)
        store(step, 0, dot(hidden_buf[...], out_buf[:, columns]))


def feed_forward(core, near, far, back, in_weight, out_weight):
    vmem = pl.BlockSpec(memory_space=pltpu.VMEM)
    anywhere = pl.BlockSpec(memory_space=pl.ANY)
    steps = in_weight.shape[0] // CHUNK
    hidden = in_weight.shape[1]
    part = jax.ShapeDtypeStruct((steps, 2 * GROUP, CHUNK // 2), BF16)
    return pl.pallas_call(
        feed_kernel,
        in_specs=[pl.BlockSpec(memory_space=pltpu.SMEM)] + [vmem] * 3 + [anywhere] * 2,
        out_specs=[vmem, vmem],
        out_shape=[part, part],
        scratch_shapes=[
            pltpu.VMEM(in_weight.shape, BF16),
            pltpu.VMEM(out_weight.shape, BF16),
            pltpu.VMEM((GROUP, steps * CHUNK), BF16),
            pltpu.VMEM((GROUP, hidden), BF16),
            pltpu.VMEM((GROUP, hidden), BF16),
            pltpu.SemaphoreType.DMA((WEIGHT_COPIES,)),
            pltpu.SemaphoreType.DMA((WEIGHT_COPIES,)),
        ],
        compiler_params=pltpu.CompilerParams(vmem_limit_bytes=46 << 20),
        cost_estimate=pl.CostEstimate(flops=1 << 20, bytes_accessed=1 << 16, transcendentals=0),
        name="feed_forward",
    )(core, near, far, back, in_weight, out_weight)


def back_kernel(core_ref, near_ref, far_ref, out_ref, back_ref, out_buf, rows_buf, sem):
    first_core = core_ref[0] == 0
    width = CHUNK // 2
    copies = []
    for chip in range(N_CHIP):
        columns = pl.ds(chip * CHUNK, CHUNK)
        copies.append(
            pltpu.make_async_copy(out_ref.at[:, columns], out_buf.at[:, columns], sem.at[chip])
        )
        copies[-1].start()
    total = 0.0
    for chip in range(N_CHIP):
        columns = pl.ds(chip * CHUNK, CHUNK)
        for half in range(2):
            lanes = pl.ds(half * width, width)
            close, away = near_ref[chip, :, lanes], far_ref[chip, :, lanes]
            rows = pl.ds(half * HALF, HALF)
            rows_buf[rows, pl.ds(chip * CHUNK, width)] = jnp.where(first_core, close, away)
            rows_buf[rows, pl.ds(chip * CHUNK + width, width)] = jnp.where(first_core, away, close)
        copies[chip].wait()
        total = total + dot(rows_buf[:, columns], out_buf[:, columns], CONTRACT_LAST)
    back_ref[...] = total


def back_terms(core, near, far, out_weight):
    vmem = pl.BlockSpec(memory_space=pltpu.VMEM)
    hidden = out_weight.shape[0]
    return pl.pallas_call(
        back_kernel,
        in_specs=[pl.BlockSpec(memory_space=pltpu.SMEM), vmem, vmem]
        + [pl.BlockSpec(memory_space=pl.ANY)],
        out_specs=vmem,
        out_shape=jax.ShapeDtypeStruct((GROUP, hidden), F32),
        scratch_shapes=[
            pltpu.VMEM(out_weight.shape, BF16),
            pltpu.VMEM((GROUP, out_weight.shape[1]), BF16),
            pltpu.SemaphoreType.DMA((N_CHIP,)),
        ],
        compiler_params=pltpu.CompilerParams(vmem_limit_bytes=46 << 20),
        cost_estimate=pl.CostEstimate(flops=1 << 20, bytes_accessed=1 << 16, transcendentals=0),
        name="back_terms",
    )(core, near, far, out_weight)


def rank_spans(lengths_ref):
    live, starts, total = [], [], 0
    for rank in range(N_DP):
        count = lengths_ref[rank, 0]
        for column in range(1, lengths_ref.shape[1]):
            count = count + lengths_ref[rank, column]
        live.append(count)
        starts.append(total)
        total = total + count
    return live, starts


def entry_of(values, rank):
    found = values[0]
    for place in range(1, N_DP):
        found = jnp.where(rank == place, values[place], found)
    return found


def first_row(group, start):
    return lax.rem(group + ROWS - start, N_DP)


def one_hot(condition):
    return condition.astype(F32).astype(BF16)


def pack_kernel(place_ref, lengths_ref, tokens_ref, cot_ref, sent_ref):
    live, starts = rank_spans(lengths_ref)
    start, own_live = entry_of(starts, place_ref[0]), entry_of(live, place_ref[0])
    row_total, width = tokens_ref.shape
    slot = lax.broadcasted_iota(jnp.int32, (SLOTS, row_total), 0)
    row = lax.broadcasted_iota(jnp.int32, (SLOTS, row_total), 1)
    for group in range(N_DP):
        wanted = slot * N_DP + first_row(group, start)
        pick = one_hot((row == wanted) & (row < own_live))
        sent_ref[group, :, pl.ds(0, width)] = dot(pick, tokens_ref[...]).astype(BF16)
        sent_ref[group, :, pl.ds(width, width)] = dot(pick, cot_ref[...]).astype(BF16)


def group_kernel(place_ref, lengths_ref, got_ref, near_ref, given_ref, cot_ref, rows_buf):
    live, starts = rank_spans(lengths_ref)
    group, core = place_ref[0], place_ref[1]
    row = lax.broadcasted_iota(jnp.int32, (GROUP, SLOTS), 0)
    slot = lax.broadcasted_iota(jnp.int32, (GROUP, SLOTS), 1)
    total = jnp.zeros((GROUP, CHUNK), F32)
    for rank in range(N_DP):
        first = first_row(group, starts[rank])
        shift = (starts[rank] + first - group) // N_DP
        pick = one_hot((row == slot + shift) & (slot * N_DP + first < live[rank]))
        total = total + dot(pick, got_ref[rank])
    rows_buf[...] = total.astype(BF16)
    width = CHUNK // 2
    left, right = pl.ds(0, width), pl.ds(width, width)
    near_ref[...] = rows_buf[pl.ds(pl.multiple_of(core * HALF, HALF), HALF), left]
    given_ref[...] = rows_buf[pl.ds(pl.multiple_of(HALF - core * HALF, HALF), HALF), left]
    cot_ref[:, left] = rows_buf[pl.ds(0, HALF), right]
    cot_ref[:, right] = rows_buf[pl.ds(HALF, HALF), right]


def spread_kernel(place_ref, lengths_ref, got_ref, mixed_ref, sent_ref, rows_buf):
    live, starts = rank_spans(lengths_ref)
    group = place_ref[0]
    total = got_ref[0].astype(F32)
    for chip in range(1, N_CHIP):
        total = total + got_ref[chip].astype(F32)
    rows_buf[...] = total.astype(BF16)
    slot = lax.broadcasted_iota(jnp.int32, (SLOTS, GROUP), 0)
    row = lax.broadcasted_iota(jnp.int32, (SLOTS, GROUP), 1)
    for rank in range(N_DP):
        first = first_row(group, starts[rank])
        shift = (starts[rank] + first - group) // N_DP
        pick = one_hot((row == slot + shift) & (slot * N_DP + first < live[rank]))
        for half in range(2):
            rows = rows_buf[pl.ds(half * GROUP, GROUP), :]
            sent_ref[rank, pl.ds(half * SLOTS, SLOTS), :] = dot(pick, rows).astype(BF16)
        sent_ref[rank, pl.ds(2 * SLOTS, GROUP), :] = mixed_ref[...]


def final_kernel(
    place_ref, lengths_ref, got_ref, rows_ref, diagonal_ref, matrix_ref, out_ref, grad_ref, step_ref
):
    live, starts = rank_spans(lengths_ref)
    start, own_live = entry_of(starts, place_ref[0]), entry_of(live, place_ref[0])
    row_total, width = out_ref.shape
    row = lax.broadcasted_iota(jnp.int32, (row_total, N_DP * SLOTS), 0)
    place = lax.broadcasted_iota(jnp.int32, (1, N_DP * SLOTS), 1)
    wanted = jnp.zeros_like(place)
    for group in range(N_DP):
        here = (place - group * SLOTS) * N_DP + first_row(group, start)
        wanted = jnp.where(place >= group * SLOTS, here, wanted)
    pick = one_hot((row == wanted) & (row < own_live))
    for target, offset in ((out_ref, 0), (grad_ref, SLOTS)):
        rows = got_ref[:, pl.ds(offset, SLOTS), :].reshape(N_DP * SLOTS, width)
        target[...] = dot(pick, rows).astype(BF16)
    mixed = got_ref[:, pl.ds(2 * SLOTS, GROUP), :].reshape(ROWS, width)
    product = dot(rows_ref[...], mixed, CONTRACT_FIRST)
    step_ref[...] = product - diagonal_ref[...] * matrix_ref[...]


def small_call(kernel, shapes, scratch, limit, *operands):
    smem = pl.BlockSpec(memory_space=pltpu.SMEM)
    vmem = pl.BlockSpec(memory_space=pltpu.VMEM)
    return pl.pallas_call(
        kernel,
        in_specs=[smem, smem] + [vmem] * (len(operands) - 2),
        out_specs=[vmem] * len(shapes),
        out_shape=shapes,
        scratch_shapes=scratch,
        compiler_params=pltpu.CompilerParams(vmem_limit_bytes=limit << 20),
        cost_estimate=pl.CostEstimate(flops=1 << 20, bytes_accessed=1 << 16, transcendentals=0),
        name=kernel.__name__,
    )(*operands)


def local(tokens, cotangent, decor_matrix, in_weight, out_weight, lengths):
    width = tokens.shape[1]
    own_rank = lax.axis_index(DP)
    core = lax.axis_index(CORE)
    core_list = core.reshape(1)
    place = jnp.stack([own_rank, core])

    def bf16_shape(*shape):
        return jax.ShapeDtypeStruct(shape, BF16)

    (sent,) = small_call(
        pack_kernel, [bf16_shape(N_DP, SLOTS, CHUNK)], [], 8, place, lengths, tokens, cotangent
    )
    got = lax.all_to_all(sent, DP, 0, 0, tiled=True)
    near_tokens, given_tokens, cot_packed = small_call(
        group_kernel,
        [bf16_shape(HALF, width), bf16_shape(HALF, width), bf16_shape(HALF, CHUNK)],
        [pltpu.VMEM((GROUP, CHUNK), BF16)],
        8,
        place,
        lengths,
        got,
    )

    pair_tokens = jnp.concatenate([near_tokens, swap_core(given_tokens)], axis=1)
    sent = jnp.broadcast_to(pair_tokens[None], (N_DP,) + pair_tokens.shape)
    got = lax.all_to_all(sent, DP, 0, 0, tiled=True)
    all_tokens = jnp.transpose(got.reshape(N_DP, N_CHIP, PART, CHUNK), (1, 0, 2, 3))

    own_high, own_low = split_bf16(decor_matrix)
    far_high = swap_core(own_high)
    pair_matrix = jnp.concatenate([own_high, far_high], axis=1)
    partial_white = dot(all_tokens.reshape(ROWS // 2, CHUNK), pair_matrix, CONTRACT_LAST)

    sent = jnp.concatenate(
        [
            partial_white.astype(BF16).reshape(N_CHIP, HALF, CHUNK),
            jnp.broadcast_to(cot_packed[None], (N_CHIP,) + cot_packed.shape),
        ],
        axis=1,
    )
    got = lax.all_to_all(sent, CHIPS, 0, 0, tiled=True)
    cot_near = got[:, HALF:]
    back_hidden = back_terms(core_list, cot_near, swap_core(cot_near), out_weight)
    white_chunk = jnp.sum(got[:, :HALF].astype(F32), axis=0).astype(BF16).reshape(N_DP, PART, CHUNK)

    white_part = lax.all_to_all(white_chunk, DP, 0, 0, tiled=True)

    sent = jnp.concatenate(
        [white_part.reshape(HALF, CHUNK), white_chunk.reshape(HALF, CHUNK)], axis=0
    )
    sent = jnp.broadcast_to(sent[None], (N_CHIP,) + sent.shape)
    got = lax.all_to_all(sent, CHIPS, 0, 0, tiled=True)

    got = lax.optimization_barrier((got, back_hidden))[0]

    def wide_rows(block):
        block = block.reshape(N_CHIP, N_DP, PART, CHUNK)
        return jnp.transpose(block, (0, 2, 1, 3)).reshape(HALF, N_DP * CHUNK)

    decor_near = wide_rows(got[:, HALF:])
    feed_near = wide_rows(got[:, :HALF])
    decor_far = swap_core(decor_near)
    feed_far = swap_core(feed_near)

    group_row = jnp.arange(GROUP, dtype=jnp.int32) * N_DP
    all_rows = (jnp.arange(N_DP, dtype=jnp.int32)[:, None] + group_row[None, :]).reshape(-1)
    row_weights = packed_weights(lengths, all_rows)
    own_weights = packed_weights(lengths, own_rank + group_row)
    white_rows, mixed_part = mixed_terms(core_list, decor_near, decor_far, own_high, own_low)
    white_rows = white_rows.reshape(ROWS, CHUNK)
    mixed_got = lax.all_to_all(mixed_part, DP, 0, 0, tiled=True)
    mixed_own = jnp.sum(mixed_got.astype(F32), axis=0)
    weighted_own = (mixed_own * own_weights[:, None]).astype(BF16)
    white_float = white_rows.astype(F32)
    diagonal = jnp.sum(row_weights[:, None] * white_float * white_float, axis=0)
    feed_near = lax.optimization_barrier((feed_near, mixed_part))[0]

    kept, given = feed_forward(
        core_list, feed_near, feed_far, back_hidden, in_weight, out_weight
    )
    given = lax.optimization_barrier((given, mixed_got))[0]
    summed = (kept.astype(F32) + swap_core(given).astype(F32)).astype(BF16)
    got = lax.all_to_all(summed, CHIPS, 0, 0, tiled=True)

    (sent,) = small_call(
        spread_kernel,
        [bf16_shape(N_DP, 2 * SLOTS + GROUP, width)],
        [pltpu.VMEM((2 * GROUP, width), BF16)],
        12,
        place,
        lengths,
        got,
        weighted_own,
    )
    got = lax.all_to_all(sent, DP, 0, 0, tiled=True)
    return tuple(
        small_call(
            final_kernel,
            [
                bf16_shape(*tokens.shape),
                bf16_shape(*tokens.shape),
                jax.ShapeDtypeStruct(decor_matrix.shape, F32),
            ],
            [],
            16,
            place,
            lengths,
            got,
            white_rows,
            diagonal[:, None],
            decor_matrix,
        )
    )


def solution(mesh):
    fine = Mesh(mesh.devices.reshape(4, 2, 2, 4, 2), ("x", "yl", "yh", "z", "core"))
    tensor = ("yh", "z", "core")
    placed = (
        P(DP, tensor),
        P(DP, tensor),
        P(DP, tensor),
        P(None, tensor),
        P(tensor, None),
        P(),
    )
    return jax.shard_map(
        local,
        mesh=fine,
        in_specs=placed,
        out_specs=(P(DP, tensor), P(DP, tensor), P(DP, tensor)),
        check_vma=False,
    )
```
